256 devices in a mesh: dp: 32 (over x, z_lo, y), section: 8 (over z_hi, core).
Axes of the slice: x: 4, y: 4, z: 8 (z_hi: 4, z_lo: 2; z = z_hi * 2 + z_lo), core: 2. Of those that a mesh axis runs over, the one named last changes fastest.
Arguments:
- latents: bfloat16 [2, 2048, 1152], P(None, 'dp'), may hold values from -6 to 6
- time_table: bfloat16 [1000, 1152], replicated, may hold values from -3 to 3
- timesteps: int32 [2], replicated, may hold values from 0 to 999
- order: int32 [2], replicated, may hold values from 0 to 1, each once
- gains: bfloat16 [8, 1152], P('section'), may hold values from 0.099609375 to 1.8984375
- w_up: bfloat16 [8, 1152, 2304], P('section', 'dp'), may hold values from -0.1875 to 0.1875
- w_down: bfloat16 [8, 2304, 1152], P('section', 'dp'), may hold values from -0.125 to 0.125
- w_join: bfloat16 [8, 1152, 1152], P('section', 'dp'), may hold values from -0.125 to 0.125
- cotangent: bfloat16 [2, 2048, 1152], P(None, 'dp'), may hold values from -0.09375 to 0.09375
Outputs:
- grad_up: float32 [8, 1152, 2304], P('section', 'dp')
- grad_down: float32 [8, 2304, 1152], P('section', 'dp')
- grad_join: float32 [8, 1152, 1152], P('section', 'dp')
The draws below stay inside these ranges and needn't reach their ends.
Inputs may be any that keep to these rules, and one draw needn't show every extreme that they name: order names each of the 2 micro-batches once.
All inputs are finite; a program needn't handle non-finite values.
Results may differ from the reference program's by a relative error of at most 0.04.
Values may be sent and summed in bfloat16 or wider, within the bound.
A program may use at most 128 MiB of HBM per device.

```python
import jax
import jax.numpy as jnp
from jax import lax

D = 1152
FFW = 2304
TOK_DEV = 64
MICRO = 2
STEPS = 1000
TOKENS = 2048
N_DP = 32
N_SECTION = 8


def level_of(stream_key, dims, cuts, smallest, top_value):
    def one(dim, parts):
        heights = jax.random.uniform(jax.random.fold_in(jax.random.fold_in(stream_key, 6), dim), (parts,), jnp.float32, smallest / len(cuts), top_value / len(cuts))
        return jnp.repeat(jnp.exp(heights), dims[dim] // parts).reshape((-1,) + (1,) * (len(dims) - dim - 1))

    loudness = one(*cuts[0])
    for cut in cuts[1:]:
        loudness = loudness * one(*cut)
    return loudness


def bell_draw(stream_key, shape, deviation, bound, split=(), dtype=jnp.bfloat16):
    array = deviation * jax.random.normal(stream_key, shape, jnp.float32)
    if split:
        array = array * level_of(stream_key, shape, split, -0.22, 0.18)
    return jnp.clip(array, -bound, bound).astype(dtype)


def setup_inputs(seed: int = 0) -> dict:
    streams_of = jax.random.split(jax.random.key(seed), 10)
    return {
        "latents": bell_draw(streams_of[0], (MICRO, TOKENS, D), 1.0, 6.0, ((1, 32),)),
        "time_table": bell_draw(streams_of[1], (STEPS, D), 0.5, 3.0),
        "timesteps": jax.random.randint(streams_of[2], (MICRO,), 0, STEPS).astype(jnp.int32),
        "order": jax.random.permutation(streams_of[3], MICRO).astype(jnp.int32),
        "gains": jnp.clip(1.0 + 0.18 * jax.random.normal(streams_of[4], (N_SECTION, D), jnp.float32), 0.099609375, 1.8984375).astype(jnp.bfloat16),
        "w_up": bell_draw(streams_of[5], (N_SECTION, D, FFW), D ** -0.5, 0.1875, ((0, 8), (1, 32))),
        "w_down": bell_draw(streams_of[6], (N_SECTION, FFW, D), FFW ** -0.5, 0.125, ((0, 8), (1, 32))),
        "w_join": bell_draw(streams_of[7], (N_SECTION, D, D), (2 * D) ** -0.5, 0.125, ((0, 8), (1, 32))),
        "cotangent": bell_draw(streams_of[8], (MICRO, TOKENS, D), (1.0 / (TOKENS * MICRO) ** 0.5), 0.09375, ((1, 32),)),
    }


EPSILON = 1e-06

def gelu_tanh(values):
    return jax.nn.gelu(values, approximate=True)

def norm_parts(inputs, gain_row):
    values = inputs.astype(jnp.float32)
    center = values - lax.optimization_barrier(jnp.mean(values, axis=-1, keepdims=True))
    inverse = lax.rsqrt(lax.optimization_barrier(jnp.mean(center * center, axis=-1, keepdims=True)) + EPSILON)
    normed = center * inverse
    scaled = (normed * gain_row.astype(jnp.float32)).astype(jnp.bfloat16)
    return (normed, inverse, scaled)

def block_forward(inputs, gain_row, up_full, down_full):
    normed, inverse, scaled = norm_parts(inputs, gain_row)
    preact = jnp.dot(scaled, up_full, preferred_element_type=jnp.float32)
    active = gelu_tanh(preact).astype(jnp.bfloat16)
    added = jnp.dot(active, down_full, preferred_element_type=jnp.float32)
    return (inputs.astype(jnp.float32) + added).astype(jnp.bfloat16)

def block_backward(inputs, gain_row, up_full, down_full, cotangent_in):
    normed, inverse, scaled = norm_parts(inputs, gain_row)
    preact = jnp.dot(scaled, up_full, preferred_element_type=jnp.float32)
    active = gelu_tanh(preact).astype(jnp.bfloat16)
    back_in = jnp.dot(cotangent_in, down_full.T, preferred_element_type=jnp.float32)
    unused, pullback = jax.vjp(gelu_tanh, preact)
    grad_pre = pullback(back_in)[0].astype(jnp.bfloat16)
    grad_scaled = jnp.dot(grad_pre, up_full.T, preferred_element_type=jnp.float32)
    grad_normed = grad_scaled * gain_row.astype(jnp.float32)
    first_mean = lax.optimization_barrier(jnp.mean(grad_normed, axis=-1, keepdims=True))
    second_mean = lax.optimization_barrier(jnp.mean(grad_normed * normed, axis=-1, keepdims=True))
    grad_mixture = (grad_normed - first_mean - normed * second_mean) * inverse
    grad_input = (cotangent_in.astype(jnp.float32) + grad_mixture).astype(jnp.bfloat16)
    return (grad_input, scaled, active, grad_pre)

def outer_sum(left_side, right_side):
    return jnp.einsum('gtd,gtf->gdf', left_side.astype(jnp.float32), right_side.astype(jnp.float32))

def settle(partial_value):
    rounded = lax.optimization_barrier(partial_value.astype(jnp.bfloat16))
    return lax.optimization_barrier(jnp.sum(rounded.astype(jnp.float32), axis=0))

def reference(latents, time_table, timesteps, order, gains, w_up, w_down, w_join, cotangent):
    sections = N_SECTION
    halfway = sections // 2
    groups = (N_DP, TOK_DEV, D)
    entries = []
    for micro_index in range(MICRO):
        mixture = latents[order[micro_index]].astype(jnp.float32) + time_table[timesteps[micro_index]].astype(jnp.float32)[None, :]
        entries.append(mixture.astype(jnp.bfloat16).reshape(groups))
    left_sides = [[None] * MICRO for block_index in range(sections)]
    block_inputs = [[None] * MICRO for block_index in range(sections)]
    skip_values = [[None] * MICRO for block_index in range(sections)]
    for micro_index in range(MICRO):
        current = entries[micro_index]
        for block_index in range(sections):
            if block_index >= halfway:
                joining = jnp.dot(current, w_join[block_index], preferred_element_type=jnp.float32)
                joining = (joining + skip_values[sections - 1 - block_index][micro_index].astype(jnp.float32)).astype(jnp.bfloat16)
                left_sides[block_index][micro_index] = current
            else:
                joining = current
            block_inputs[block_index][micro_index] = joining
            current = block_forward(joining, gains[block_index], w_up[block_index], w_down[block_index])
            if block_index < halfway:
                skip_values[block_index][micro_index] = jnp.dot(current, w_join[block_index], preferred_element_type=jnp.float32).astype(jnp.bfloat16)
                left_sides[block_index][micro_index] = current
    carried = [cotangent[micro_index].reshape(groups) for micro_index in range(MICRO)]
    returned = [[None] * MICRO for block_index in range(sections)]
    up_list = [None] * sections
    down_list = [None] * sections
    join_list = [None] * sections
    for block_index in range(sections - 1, -1, -1):
        partial_up = jnp.zeros((N_DP, D, FFW), jnp.float32)
        partial_down = jnp.zeros((N_DP, FFW, D), jnp.float32)
        partial_join = jnp.zeros((N_DP, D, D), jnp.float32)
        passed = []
        for micro_index in range(MICRO):
            if block_index < halfway:
                turned = returned[block_index][micro_index]
                extra = jnp.dot(turned, w_join[block_index].T, preferred_element_type=jnp.float32)
                cotangent_in = (carried[micro_index].astype(jnp.float32) + extra).astype(jnp.bfloat16)
            else:
                cotangent_in = carried[micro_index]
            grad_input, scaled, active, grad_pre = block_backward(block_inputs[block_index][micro_index], gains[block_index], w_up[block_index], w_down[block_index], cotangent_in)
            if block_index >= halfway:
                right_side = grad_input
                returned[sections - 1 - block_index][micro_index] = grad_input
                passed.append(jnp.dot(grad_input, w_join[block_index].T, preferred_element_type=jnp.float32).astype(jnp.bfloat16))
            else:
                right_side = turned
                passed.append(grad_input)
            partial_up = partial_up + outer_sum(scaled, grad_pre)
            partial_down = partial_down + outer_sum(active, cotangent_in)
            partial_join = partial_join + outer_sum(left_sides[block_index][micro_index], right_side)
        carried = passed
        up_list[block_index] = settle(partial_up)
        down_list[block_index] = settle(partial_down)
        join_list[block_index] = settle(partial_join)
    return (jnp.stack(up_list), jnp.stack(down_list), jnp.stack(join_list))
```

```python
import functools

import jax
import jax.numpy as jnp
from jax import lax
from jax.experimental import pallas as pl
from jax.experimental.pallas import tpu as pltpu
from jax.sharding import PartitionSpec as P

BF = jnp.bfloat16
F32 = jnp.float32
EPSILON = 1e-06
MESH = pl.DeviceIdType.MESH
D = 1152
FFW = 2304
ROWS = 64
DIRS = ((1, 8), (-1, 7))
PART = (((0, 5), (5, 4)), ((0, 4), (4, 5)), ((0, 4), (4, 5)))
UNIT = ((4, FFW), (8, D), (4, D))
GELU_C = 0.7978845608028654
GELU_A = 0.044715


def rem(a, b):
    return lax.rem(a, jnp.int32(b))


def div(a, b):
    return lax.div(a, jnp.int32(b))


def cycle_xy(h, t):
    a = div(t, 4)
    b = rem(t + 16 - a, 4)
    return (a, b) if h == 0 else (b, a)


def dot(a, b):
    return jnp.dot(a, b, preferred_element_type=F32)


def dot_nt(a, b):
    return lax.dot_general(a, b, (((1,), (1,)), ((), ())), preferred_element_type=F32)


def await_bytes(ref, sem):
    pltpu.make_async_copy(ref, ref, sem).wait()


def kernel(
    up_in, dn_in, jn_in, gain_in, ent_in, cot_in,
    up_out, dn_out, jn_out,
    g_up, g_dn, g_jn, w_up, w_dn, w_jn, rx_up, rx_dn, rx_jn, rr_up, rr_dn, rr_jn,
    fo_up, fo_dn, fo_jn, gain, hin, skin, cin, tin, u_s, hout, skout, cout, gout,
    scaled_s, active_s, dg_s, gp_s, e_s, normed_s, inv_s, right_s, lt, at,
    swap_sem, swap_send, io_send, ag_recv, ag_send, f_recv, f_send,
    act_recv, act_send, x_recv, x_send, rs_recv, rs_send, o_recv, o_send,
):
    q = lax.axis_index("dp")
    s = lax.axis_index("section")
    x, zl, y = div(q, 8), rem(div(q, 4), 2), rem(q, 4)
    zh, c = div(s, 2), rem(s, 2)
    z = 2 * zh + zl
    deep = z >= 4

    def device(xx, yy, zz, cc):
        return (xx * 8 + rem(zz, 2) * 4 + yy, div(zz, 2) * 2 + cc)

    partner = device(x, y, z, 1 - c)
    z_up = device(x, y, rem(z + 1, 8), c)
    z_down = device(x, y, rem(z + 7, 8), c)
    mirror = device(x, y, 7 - z, c)
    swap = device(x, y, 2 * zh + c, zl)
    stays = zl == c
    pos = (4 * x + rem(x + y, 4), 4 * y + rem(x + y, 4))

    def neighbour(h, d):
        xx, yy = cycle_xy(h, rem(pos[h] + 16 + d, 16))
        return device(xx, yy, z, c)

    def slot_of(h, t, cls):
        xx, yy = cycle_xy(h, t)
        return xx * 8 + cls * 4 + yy

    ring = tuple(tuple(neighbour(h, d) for d, _ in DIRS) for h in range(2))
    other = device(x, y, rem(z, 2) * 0 + 2 * zh + 1 - zl, 1 - c)

    barrier = pltpu.get_barrier_semaphore()
    greet = [ring[0][0], ring[0][1], ring[1][0], ring[1][1], partner, z_up, z_down, mirror, other]
    for peer in greet:
        pl.semaphore_signal(barrier, inc=1, device_id=peer, device_id_type=MESH)
    pl.semaphore_wait(barrier, len(greet))

    gs = (g_up, g_dn, g_jn)
    rxs = (rx_up, rx_dn, rx_jn)
    rrs = (rr_up, rr_dn, rr_jn)
    fos = (fo_up, fo_dn, fo_jn)
    outs = (up_out, dn_out, jn_out)

    def remote(src, dst, send, recv, dev):
        return pltpu.make_async_remote_copy(
            src_ref=src, dst_ref=dst, send_sem=send, recv_sem=recv, device_id=dev, device_id_type=MESH
        )

    def swap_copy(src, dst, send, recv):
        @pl.when(stays)
        def _():
            pltpu.make_async_copy(src, dst, recv).start()

        @pl.when(jnp.logical_not(stays))
        def _():
            remote(src, dst, send, recv, swap).start()

    def swap_sent(src, send):
        @pl.when(jnp.logical_not(stays))
        def _():
            await_bytes(src, send)

    ins = (up_in, dn_in, jn_in)
    for m in range(3):
        swap_copy(ins[m], gs[m].at[pl.ds(9 * q, 9)], swap_send.at[m], swap_sem.at[m])
    swap_copy(gain_in, gain, swap_send.at[3], swap_sem.at[3])
    gives_entry = (zh == 0) & (c == 0)
    gives_cot = (zh == 3) & (c == 1)

    @pl.when(gives_entry)
    def _():
        for i in range(2):
            swap_copy(ent_in.at[i], hin.at[i], io_send.at[0, i], act_recv.at[0, i])

    @pl.when(gives_cot)
    def _():
        for i in range(2):
            swap_copy(cot_in.at[i], cin.at[i], io_send.at[1, i], act_recv.at[2, i])

    own = x * 8 + c * 4 + y
    for m in range(3):
        await_bytes(gs[m].at[pl.ds(9 * own, 9)], swap_sem.at[m])

    def chunk(m, h, t):
        off, cnt = PART[m][h]
        return gs[m].at[pl.ds(9 * slot_of(h, t, c) + off, cnt)]

    def ag_step(k, _):
        for m in range(3):
            for h in range(2):
                for di, (d, n) in enumerate(DIRS):
                    @pl.when(k < n)
                    def _():
                        ref = chunk(m, h, rem(pos[h] + 16 - d * k, 16))

                        @pl.when(k > 0)
                        def _():
                            await_bytes(ref, ag_recv.at[m, h, di, lax.max(k - 1, 0)])

                        remote(ref, ref, ag_send.at[m], ag_recv.at[m, h, di, k], ring[h][di]).start()
                        if di == 0:
                            remote(ref, ref, f_send.at[m], f_recv.at[m], partner).start()
                        else:
                            @pl.when(k > 0)
                            def _():
                                remote(ref, ref, f_send.at[m], f_recv.at[m], partner).start()
        return 0

    lax.fori_loop(0, 8, ag_step, 0)
    for m in range(3):
        for h in range(2):
            for di, (d, n) in enumerate(DIRS):
                ref = chunk(m, h, rem(pos[h] + 16 - d * n, 16))
                await_bytes(ref, ag_recv.at[m, h, di, n - 1])
                remote(ref, ref, f_send.at[m], f_recv.at[m], partner).start()
    for m in range(3):
        await_bytes(gs[m].at[pl.ds(0, 144)], f_recv.at[m])

    def conv_up(t, _):
        w_up[pl.ds(pl.multiple_of(t * 16, 16), 16), :] = g_up[pl.ds(t * 4, 4)].reshape(16, FFW)
        return 0

    def conv_dn(t, _):
        w_dn[pl.ds(pl.multiple_of(t * 32, 32), 32), :] = g_dn[pl.ds(t * 4, 4)].reshape(32, D)
        return 0

    def conv_jn(t, _):
        w_jn[pl.ds(pl.multiple_of(t * 16, 16), 16), :] = g_jn[pl.ds(t * 4, 4)].reshape(16, D)
        return 0

    lax.fori_loop(0, 72, conv_up, 0, unroll=2)
    lax.fori_loop(0, 72, conv_dn, 0, unroll=2)
    lax.fori_loop(0, 72, conv_jn, 0, unroll=2)
    await_bytes(gain, swap_sem.at[3])

    def half(i):
        return pl.ds(pl.multiple_of(i * ROWS, ROWS), ROWS)

    def forward(i, _):
        await_bytes(hin.at[i], act_recv.at[0, i])

        @pl.when(deep)
        def _():
            joined = dot(hin[i], w_jn[...])
            await_bytes(skin.at[i], act_recv.at[1, i])
            u_s[i] = (joined + skin[i].astype(F32)).astype(BF)

        @pl.when(jnp.logical_not(deep))
        def _():
            u_s[i] = hin[i]

        values = u_s[i].astype(F32)
        center = values - jnp.mean(values, axis=-1, keepdims=True)
        inverse = lax.rsqrt(jnp.mean(center * center, axis=-1, keepdims=True) + EPSILON)
        normed = center * inverse
        normed_s[i] = normed
        inv_s[i] = jnp.broadcast_to(inverse, (ROWS, 128))
        scaled_s[half(i), :] = (normed * gain[0:1, :]).astype(BF)
        pre = dot(scaled_s[half(i), :], w_up[...])
        square = pre * pre
        bent = jnp.tanh(GELU_C * (pre + GELU_A * (square * pre)))
        grown = 0.5 * (1.0 + bent)
        active_s[half(i), :] = (pre * grown).astype(BF)
        dg_s[i] = grown + 0.5 * pre * (1.0 - bent * bent) * (GELU_C * (1.0 + 3.0 * GELU_A * square))

        @pl.when(z < 7)
        def _():
            hout[i] = (u_s[i].astype(F32) + dot(active_s[half(i), :], w_dn[...])).astype(BF)
            remote(hout.at[i], hin.at[i], act_send.at[0, i], act_recv.at[0, i], z_up).start()

        @pl.when(jnp.logical_not(deep))
        def _():
            skout[i] = dot(hout[i], w_jn[...]).astype(BF)
            remote(skout.at[i], skin.at[i], act_send.at[1, i], act_recv.at[1, i], mirror).start()
        return 0

    lax.fori_loop(0, 2, forward, 0)

    def backward(i, _):
        @pl.when(jnp.logical_not(deep))
        def _():
            await_bytes(tin.at[i], act_recv.at[3, i])
            turned = dot_nt(tin[i], w_jn[...])
            await_bytes(cin.at[i], act_recv.at[2, i])
            e_s[half(i), :] = (cin[i].astype(F32) + turned).astype(BF)

        @pl.when(deep)
        def _():
            await_bytes(cin.at[i], act_recv.at[2, i])
            e_s[half(i), :] = cin[i]

        back_in = dot_nt(e_s[half(i), :], w_dn[...])
        gp_s[half(i), :] = (dg_s[i] * back_in).astype(BF)

        @pl.when(z > 0)
        def _():
            grad_normed = dot_nt(gp_s[half(i), :], w_up[...]) * gain[0:1, :]
            normed = normed_s[i]
            first = jnp.mean(grad_normed, axis=-1, keepdims=True)
            second = jnp.mean(grad_normed * normed, axis=-1, keepdims=True)
            mixture = (grad_normed - first - normed * second) * inv_s[i][:, 0:1]
            gout[i] = (e_s[half(i), :].astype(F32) + mixture).astype(BF)

            @pl.when(deep)
            def _():
                remote(gout.at[i], tin.at[i], act_send.at[3, i], act_recv.at[3, i], mirror).start()
                cout[i] = dot_nt(gout[i], w_jn[...]).astype(BF)
                remote(cout.at[i], cin.at[i], act_send.at[2, i], act_recv.at[2, i], z_down).start()

            @pl.when(jnp.logical_not(deep))
            def _():
                remote(gout.at[i], cin.at[i], act_send.at[2, i], act_recv.at[2, i], z_down).start()
        return 0

    lax.fori_loop(0, 2, backward, 0)

    for m in range(3):
        await_bytes(gs[m].at[pl.ds(0, 135)], ag_send.at[m])
        await_bytes(gs[m].at[pl.ds(0, 144)], f_send.at[m])

    def partials(m, left, right, rows):
        def to_partner(j, _):
            t = 2 * j + 1 - c
            units = pl.ds(36 * t, 36)
            part = dot(left[pl.ds(pl.multiple_of(t * rows, rows), rows), :], right[...])
            gs[m][units] = part.reshape((36,) + UNIT[m]).astype(BF)
            remote(gs[m].at[units], rxs[m].at[pl.ds(36 * j, 36)], x_send.at[m], x_recv.at[m], partner).start()
            return 0

        def to_self(j, _):
            t = 2 * j + c
            part = dot(left[pl.ds(pl.multiple_of(t * rows, rows), rows), :], right[...])
            gs[m][pl.ds(36 * t, 36)] = part.reshape((36,) + UNIT[m]).astype(BF)
            return 0

        lax.fori_loop(0, 4, to_partner, 0)
        lax.fori_loop(0, 4, to_self, 0)

    at[...] = active_s[...].T
    partials(1, at, e_s, 288)
    lt[...] = scaled_s[...].T
    partials(0, lt, gp_s, 144)

    @pl.when(deep)
    def _():
        lt[...] = hin[...].reshape(128, D).T
        right_s[...] = gout[...].reshape(128, D)

    @pl.when(jnp.logical_not(deep))
    def _():
        lt[...] = hout[...].reshape(128, D).T
        right_s[...] = tin[...].reshape(128, D)

    partials(2, lt, right_s, 144)
    for m in range(3):
        await_bytes(rxs[m].at[...], x_recv.at[m])

    def landing(m, h, di, k):
        cnt = PART[m][h][1]
        start = (0 if h == 0 else 15 * PART[m][0][1]) + (0 if di == 0 else 8 * cnt)
        return pl.ds(start + k * cnt, cnt)

    def rs_step(k, _):
        for m in (1, 0, 2):
            for h in range(2):
                off, cnt = PART[m][h]
                for di, (d, n) in enumerate(DIRS):
                    @pl.when(k < n)
                    def _():
                        xx, yy = cycle_xy(h, rem(pos[h] + 16 - d * (n - k), 16))
                        mine = pl.ds(9 * (xx * 8 + c * 4 + yy) + off, cnt)
                        total = gs[m][mine].astype(F32) + rxs[m][pl.ds(9 * (4 * xx + yy) + off, cnt)].astype(F32)

                        @pl.when(k == 0)
                        def _():
                            gs[m][mine] = total.astype(BF)

                        @pl.when(k > 0)
                        def _():
                            before = landing(m, h, di, lax.max(k - 1, 0))
                            await_bytes(rrs[m].at[before], rs_recv.at[m, h, di, lax.max(k - 1, 0)])
                            gs[m][mine] = (total + rrs[m][before].astype(F32)).astype(BF)

                        remote(
                            gs[m].at[mine], rrs[m].at[landing(m, h, di, k)],
                            rs_send.at[m], rs_recv.at[m, h, di, k], ring[h][1 - di],
                        ).start()
        return 0

    lax.fori_loop(0, 8, rs_step, 0)
    for m in (1, 0, 2):
        for h in range(2):
            off, cnt = PART[m][h]
            mine = pl.ds(9 * own + off, cnt)
            total = gs[m][mine].astype(F32) + rxs[m][pl.ds(9 * (4 * x + y) + off, cnt)].astype(F32)
            for di, (d, n) in enumerate(DIRS):
                last = landing(m, h, di, n - 1)
                await_bytes(rrs[m].at[last], rs_recv.at[m, h, di, n - 1])
                total = total + rrs[m][last].astype(F32)
            gs[m][mine] = total.astype(BF)
        swap_copy(gs[m].at[pl.ds(9 * own, 9)], fos[m], o_send.at[m], o_recv.at[m])

    for m in (1, 0, 2):
        await_bytes(fos[m], o_recv.at[m])
        outs[m][...] = fos[m][...].astype(F32)

    for m in range(3):
        swap_sent(ins[m], swap_send.at[m])
        swap_sent(fos[m], o_send.at[m])
        await_bytes(gs[m].at[pl.ds(0, 144)], x_send.at[m])
        await_bytes(gs[m].at[pl.ds(0, 135)], rs_send.at[m])
    swap_sent(gain_in, swap_send.at[3])

    @pl.when(gives_entry)
    def _():
        for i in range(2):
            swap_sent(ent_in.at[i], io_send.at[0, i])

    @pl.when(gives_cot)
    def _():
        for i in range(2):
            swap_sent(cot_in.at[i], io_send.at[1, i])

    for i in range(2):
        @pl.when(z < 7)
        def _():
            await_bytes(hout.at[i], act_send.at[0, i])

        @pl.when(jnp.logical_not(deep))
        def _():
            await_bytes(skout.at[i], act_send.at[1, i])

        @pl.when(z > 0)
        def _():
            await_bytes(cout.at[i], act_send.at[2, i])

        @pl.when(deep)
        def _():
            await_bytes(gout.at[i], act_send.at[3, i])


def vm(*shape, dtype=BF):
    return pltpu.VMEM(shape, dtype)


def local(latents, time_table, timesteps, order, gains, w_up, w_down, w_join, cotangent):
    entry = (
        latents[order].astype(F32) + time_table[timesteps].astype(F32)[:, None, :]
    ).astype(BF)
    gain = jnp.broadcast_to(gains.astype(F32), (8, D))
    act = (2, ROWS, D)
    dma = pltpu.SemaphoreType.DMA
    scratch = (
        [vm(288, *u) for u in UNIT]
        + [vm(D, FFW), vm(FFW, D), vm(D, D)]
        + [vm(144, *u) for u in UNIT]
        + [vm(135, *u) for u in UNIT]
        + [vm(9, *u) for u in UNIT]
        + [vm(8, D, dtype=F32)]
        + [vm(*act) for _ in range(9)]
        + [
            vm(2 * ROWS, D), vm(2 * ROWS, FFW), vm(2, ROWS, FFW, dtype=F32), vm(2 * ROWS, FFW), vm(2 * ROWS, D),
            vm(*act, dtype=F32), vm(2, ROWS, 128, dtype=F32), vm(2 * ROWS, D), vm(D, 2 * ROWS), vm(FFW, 2 * ROWS),
        ]
        + [
            dma((4,)), dma((4,)), dma((2, 2)), dma((3, 2, 2, 8)), dma((3,)), dma((3,)), dma((3,)),
            dma((4, 2)), dma((4, 2)), dma((3,)), dma((3,)), dma((3, 2, 2, 8)), dma((3,)), dma((3,)), dma((3,)),
        ]
    )
    spec = pl.BlockSpec(memory_space=pltpu.VMEM)
    up, down, join = pl.pallas_call(
        kernel,
        out_shape=[jax.ShapeDtypeStruct((9,) + u, F32) for u in UNIT],
        in_specs=[spec] * 6,
        out_specs=[spec] * 3,
        scratch_shapes=scratch,
        compiler_params=pltpu.CompilerParams(
            collective_id=0, has_side_effects=True, vmem_limit_bytes=58 * 2**20
        ),
        name="blocks",
    )(
        w_up.reshape((9,) + UNIT[0]), w_down.reshape((9,) + UNIT[1]), w_join.reshape((9,) + UNIT[2]),
        gain, entry, cotangent,
    )
    return up.reshape(1, 36, FFW), down.reshape(1, 72, D), join.reshape(1, 36, D)


def solution(mesh):
    in_specs = (
        P(None, "dp", None),
        P(),
        P(),
        P(),
        P("section", None),
        P("section", "dp", None),
        P("section", "dp", None),
        P("section", "dp", None),
        P(None, "dp", None),
    )
    out_specs = (P("section", "dp", None), P("section", "dp", None), P("section", "dp", None))
    return jax.shard_map(local, mesh=mesh, in_specs=in_specs, out_specs=out_specs, check_vma=False)
```

```python
import jax
import jax.numpy as jnp
from jax import lax
from jax.experimental import pallas as pl
from jax.experimental.pallas import tpu as pltpu
from jax.sharding import PartitionSpec as P

BF = jnp.bfloat16
F32 = jnp.float32
EPSILON = 1e-06
MESH = pl.DeviceIdType.MESH
D = 1152
FFW = 2304
ROWS = 32
MICROS = 4
EARLY = 2
CHUNKS = ((0, 512), (512, 640))
PART = (((0, 5, 1), (5, 4, -1)), ((0, 4, -1), (4, 5, 1)), ((0, 4, 1), (4, 5, -1)))
UNIT = ((4, FFW), (8, D), (4, D))
GELU_C = 0.7978845608028654
GELU_A = 0.044715


def rem(a, b):
    return lax.rem(a, jnp.int32(b))


def div(a, b):
    return lax.div(a, jnp.int32(b))


def dot(a, b):
    return jnp.dot(a, b, preferred_element_type=F32)


def await_bytes(ref, sem):
    pltpu.make_async_copy(ref, ref, sem).wait()


def kernel(
    up_in, dn_in, jn_in, gain_in, ent_in, cot_in,
    up_out, dn_out, jn_out,
    g_up, g_dn, g_jn, w_up, w_dn, w_jn, wt_up, wt_dn, wt_jn, rx_up, rx_dn, rx_jn, rr_up, rr_dn, rr_jn,
    st_up, st_dn, st_jn, st_gain, gain, hin, skin, cin, tin, u_s, hout, skout, cout, gout,
    scaled_s, active_s, dg_s, gp_s, e_s, mean_s, inv_s, turned_s, right_s, lt, at,
    swap_sem, swap_send, io_send, ag_recv, ag_send, f_recv, f_send,
    h_recv, h_send, c_recv, c_send, act_recv, act_send, x_recv, x_send, rs_recv, rs_send, o_recv, o_send,
):
    q = lax.axis_index("dp")
    s = lax.axis_index("section")
    x, zl, y = div(q, 8), rem(div(q, 4), 2), rem(q, 4)
    zh, c = div(s, 2), rem(s, 2)
    z = 2 * zh + zl
    deep = z >= 4

    def device(xx, yy, zz, cc):
        return (xx * 8 + rem(zz, 2) * 4 + yy, div(zz, 2) * 2 + cc)

    partner = device(x, y, z, 1 - c)
    z_up = device(x, y, rem(z + 1, 8), c)
    z_down = device(x, y, rem(z + 7, 8), c)
    mirror = device(x, y, 7 - z, c)
    swap = device(x, y, 2 * zh + c, zl)
    stays = zl == c

    def along(axis, step):
        if axis == 0:
            return device(rem(x + 4 + step, 4), y, z, c)
        return device(x, rem(y + 4 + step, 4), z, c)

    other = device(x, y, 2 * zh + 1 - zl, 1 - c)

    def owner(h, d, i, j):
        back, side = 8 - d * i, 8 - d * j
        if h == 0:
            return rem(x + side, 4), rem(y + back, 4)
        return rem(x + back, 4), rem(y + side, 4)

    gs = (g_up, g_dn, g_jn)
    rxs = (rx_up, rx_dn, rx_jn)
    rrs = (rr_up, rr_dn, rr_jn)
    outs = (up_out, dn_out, jn_out)

    def remote(src, dst, send, recv, dev):
        return pltpu.make_async_remote_copy(
            src_ref=src, dst_ref=dst, send_sem=send, recv_sem=recv, device_id=dev, device_id_type=MESH
        )

    def swap_copy(src, dst, send, recv):
        @pl.when(stays)
        def _():
            pltpu.make_async_copy(src, dst, recv).start()

        @pl.when(jnp.logical_not(stays))
        def _():
            remote(src, dst, send, recv, swap).start()

    def swap_sent(src, send):
        @pl.when(jnp.logical_not(stays))
        def _():
            await_bytes(src, send)

    ins = (st_up, st_dn, st_jn)
    st_up[...] = up_in[...].reshape((9,) + UNIT[0])
    st_dn[...] = dn_in[...].reshape((9,) + UNIT[1])
    st_jn[...] = jn_in[...].reshape((9,) + UNIT[2])
    st_gain[...] = jnp.broadcast_to(gain_in[...].astype(F32), (8, D))

    barrier = pltpu.get_barrier_semaphore()
    greet = [along(0, 1), along(0, -1), along(1, 1), along(1, -1), partner, z_up, z_down, mirror, other]
    for peer in greet:
        pl.semaphore_signal(barrier, inc=1, device_id=peer, device_id_type=MESH)
    pl.semaphore_wait(barrier, len(greet))

    for m in range(3):
        swap_copy(ins[m], gs[m].at[pl.ds(9 * q, 9)], swap_send.at[m], swap_sem.at[m])
    swap_copy(st_gain, gain, swap_send.at[3], swap_sem.at[3])
    gives_entry = (zh == 0) & (c == 0)
    gives_cot = (zh == 3) & (c == 1)

    @pl.when(gives_entry)
    def _():
        for i in range(MICROS):
            for n, (lo, size) in enumerate(CHUNKS):
                cols = pl.ds(lo, size)
                swap_copy(ent_in.at[i, :, cols], hin.at[i, :, cols], io_send.at[0, i, n], h_recv.at[i, n])

    @pl.when(gives_cot)
    def _():
        for i in range(MICROS):
            for n, (lo, size) in enumerate(CHUNKS):
                cols = pl.ds(lo, size)
                swap_copy(cot_in.at[i, :, cols], cin.at[i, :, cols], io_send.at[1, i, n], c_recv.at[i, n])

    own = x * 8 + c * 4 + y
    halves = [(m, h) for m in range(3) for h in range(2)]

    def piece(m, h, i, j):
        off, cnt, d = PART[m][h]
        xx, yy = owner(h, d, i, j)
        return gs[m].at[pl.ds(9 * (xx * 8 + c * 4 + yy) + off, cnt)]

    def spread(m, ref, axis, step, recv):
        remote(ref, ref, ag_send.at[m], recv, along(axis, step)).start()

    def to_partner(m, ref):
        remote(ref, ref, f_send.at[m], f_recv.at[m], partner).start()

    def first_axis(t, _):
        i = t + div(t, 2) * (5 - 2 * t)
        for m, h in halves:
            d = PART[m][h][2]
            f = 1 - h
            ref = piece(m, h, i, 0)

            @pl.when(i == 0)
            def _():
                if h == 0:
                    await_bytes(gs[m].at[pl.ds(9 * own, 9)], swap_sem.at[m])
                spread(m, ref, f, d, ag_recv.at[m, h, 1])
                spread(m, ref, f, -d, ag_recv.at[m, h, 3])

            @pl.when(i > 0)
            def _():
                await_bytes(ref, ag_recv.at[m, h, i])

            @pl.when(i == 1)
            def _():
                spread(m, ref, f, d, ag_recv.at[m, h, 2])

            spread(m, ref, 1 - f, d, ag_recv.at[m, h, 4 + i])
            spread(m, ref, 1 - f, -d, ag_recv.at[m, h, 12 + i])
            to_partner(m, ref)
        return 0

    def second_axis(t, _):
        i = t + div(t, 2) * (5 - 2 * t)
        for m, h in halves:
            d = PART[m][h][2]
            ref = piece(m, h, i, 1)
            await_bytes(ref, ag_recv.at[m, h, 4 + i])
            spread(m, ref, h, d, ag_recv.at[m, h, 8 + i])
            to_partner(m, ref)
            ref = piece(m, h, i, 3)
            await_bytes(ref, ag_recv.at[m, h, 12 + i])
            to_partner(m, ref)
        return 0

    def last_hop(t, _):
        i = t + div(t, 2) * (5 - 2 * t)
        for m, h in halves:
            ref = piece(m, h, i, 2)
            await_bytes(ref, ag_recv.at[m, h, 8 + i])
            to_partner(m, ref)
        return 0

    lax.fori_loop(0, 4, first_axis, 0)
    lax.fori_loop(0, 4, second_axis, 0)
    lax.fori_loop(0, 4, last_hop, 0)
    for m in range(3):
        await_bytes(gs[m].at[pl.ds(0, 144)], f_recv.at[m])

    def conv_up(t, _):
        w_up[pl.ds(pl.multiple_of(t * 16, 16), 16), :] = g_up[pl.ds(t * 4, 4)].reshape(16, FFW)
        return 0

    def conv_dn(t, _):
        w_dn[pl.ds(pl.multiple_of(t * 32, 32), 32), :] = g_dn[pl.ds(t * 4, 4)].reshape(32, D)
        return 0

    def conv_jn(t, _):
        w_jn[pl.ds(pl.multiple_of(t * 16, 16), 16), :] = g_jn[pl.ds(t * 4, 4)].reshape(16, D)
        return 0

    lax.fori_loop(0, 72, conv_up, 0, unroll=2)
    lax.fori_loop(0, 72, conv_dn, 0, unroll=2)
    lax.fori_loop(0, 72, conv_jn, 0, unroll=2)
    await_bytes(gain, swap_sem.at[3])

    def rows(i):
        return pl.ds(pl.multiple_of(i * ROWS, ROWS), ROWS)

    def transposes():
        def turn(src, dst, n):
            def one(i, _):
                block = pl.ds(pl.multiple_of(i * 128, 128), 128)
                dst[:, block] = src[block, :].T
                return 0

            lax.fori_loop(0, n, one, 0)

        turn(w_dn, wt_dn, 18)
        turn(w_up, wt_up, 9)
        turn(w_jn, wt_jn, 9)

    def forward(i, _):
        for n, (lo, size) in enumerate(CHUNKS):
            await_bytes(hin.at[i, :, pl.ds(lo, size)], h_recv.at[i, n])

        @pl.when(deep)
        def _():
            joined = dot(hin[i], w_jn[...])
            await_bytes(skin.at[i], act_recv.at[0, i])
            u_s[i] = (joined + skin[i].astype(F32)).astype(BF)

        @pl.when(jnp.logical_not(deep))
        def _():
            u_s[i] = hin[i]

        values = u_s[i].astype(F32)
        middle = jnp.mean(values, axis=-1, keepdims=True)
        center = values - middle
        inverse = lax.rsqrt(jnp.mean(center * center, axis=-1, keepdims=True) + EPSILON)
        normed = center * inverse
        mean_s[i] = jnp.broadcast_to(middle, (ROWS, 128))
        inv_s[i] = jnp.broadcast_to(inverse, (ROWS, 128))
        scaled_s[rows(i), :] = (normed * gain[0:1, :]).astype(BF)
        pre = dot(scaled_s[rows(i), :], w_up[...])
        square = pre * pre
        bent = jnp.tanh(GELU_C * (pre + GELU_A * (square * pre)))
        grown = 0.5 * (1.0 + bent)
        active_s[rows(i), :] = (pre * grown).astype(BF)
        dg_s[i] = grown + 0.5 * pre * (1.0 - bent * bent) * (GELU_C * (1.0 + 3.0 * GELU_A * square))

        @pl.when(z < 7)
        def _():
            for n, (lo, size) in enumerate(CHUNKS):
                cols = pl.ds(lo, size)
                grown_by = dot(active_s[rows(i), :], w_dn[:, cols])
                hout[i, :, cols] = (u_s[i, :, cols].astype(F32) + grown_by).astype(BF)
                remote(hout.at[i, :, cols], hin.at[i, :, cols], h_send.at[i, n], h_recv.at[i, n], z_up).start()

        @pl.when(jnp.logical_not(deep))
        def _():
            skout[i] = dot(hout[i], w_jn[...]).astype(BF)
            remote(skout.at[i], skin.at[i], act_send.at[0, i], act_recv.at[0, i], mirror).start()
        return 0

    @pl.when(deep)
    def _():
        transposes()

    lax.fori_loop(0, MICROS, forward, 0)

    @pl.when(jnp.logical_not(deep))
    def _():
        transposes()

    for m in range(3):
        await_bytes(gs[m].at[pl.ds(0, 135)], ag_send.at[m])
        await_bytes(gs[m].at[pl.ds(0, 144)], f_send.at[m])

    def partials(m, left, right, size, to_partner):
        def one(j, _):
            t = 2 * j + (1 - c if to_partner else c)
            units = pl.ds(36 * t, 36)
            part = dot(left[pl.ds(pl.multiple_of(t * size, size), size), :], right[...])
            gs[m][units] = part.reshape((36,) + UNIT[m]).astype(BF)
            if to_partner:
                remote(gs[m].at[units], rxs[m].at[pl.ds(36 * j, 36)], x_send.at[m], x_recv.at[m], partner).start()
            return 0

        lax.fori_loop(0, 4, one, 0)

    def join_partials():
        @pl.when(deep)
        def _():
            lt[...] = hin[...].reshape(128, D).T
            right_s[...] = gout[...].reshape(128, D)

        @pl.when(jnp.logical_not(deep))
        def _():
            lt[...] = hout[...].reshape(128, D).T
            right_s[...] = tin[...].reshape(128, D)

        partials(2, lt, right_s, 144, True)
        partials(2, lt, right_s, 144, False)

    def reduce_scatter(which):
        parts = [(m, h) for m in which for h in range(2)]
        for m in which:
            await_bytes(rxs[m].at[...], x_recv.at[m])

        def rows_of(m, h, i, j):
            off, cnt, d = PART[m][h]
            xx, yy = owner(h, d, i, j)
            return pl.ds(9 * (xx * 8 + c * 4 + yy) + off, cnt), pl.ds(9 * (4 * xx + yy) + off, cnt)

        def landing(m, h, n):
            cnt = PART[m][h][1]
            return pl.ds((0 if h == 0 else 15 * PART[m][0][1]) + n * cnt, cnt)

        def arrived(m, h, n):
            spot = landing(m, h, n)
            await_bytes(rrs[m].at[spot], rs_recv.at[m, h, n])
            return rrs[m][spot].astype(F32)

        def settle(m, h, i, j, slots):
            mine, theirs = rows_of(m, h, i, j)
            total = gs[m][mine].astype(F32) + rxs[m][theirs].astype(F32)
            for n in slots:
                total = total + arrived(m, h, n)
            gs[m][mine] = total.astype(BF)
            return gs[m].at[mine]

        def send(m, h, ref, axis, step, n):
            remote(
                ref, rrs[m].at[landing(m, h, n)], rs_send.at[m], rs_recv.at[m, h, n], along(axis, step)
            ).start()

        def far(i, _):
            for m, h in parts:
                send(m, h, settle(m, h, i, 2, ()), h, -PART[m][h][2], i)
            return 0

        def near(i, _):
            for m, h in parts:
                send(m, h, settle(m, h, i, 3, ()), h, PART[m][h][2], 4 + i)
            return 0

        def middle(i, _):
            for m, h in parts:
                send(m, h, settle(m, h, i, 1, (i,)), h, -PART[m][h][2], 8 + i)
            return 0

        lax.fori_loop(0, 4, far, 0)
        lax.fori_loop(0, 4, near, 0)
        lax.fori_loop(0, 4, middle, 0)
        for m, h in parts:
            send(m, h, settle(m, h, 2, 0, (6, 10)), 1 - h, -PART[m][h][2], 12)
        for m, h in parts:
            send(m, h, settle(m, h, 3, 0, (7, 11)), 1 - h, PART[m][h][2], 14)
        for m, h in parts:
            send(m, h, settle(m, h, 1, 0, (5, 9, 12)), 1 - h, -PART[m][h][2], 13)
        for m, h in parts:
            settle(m, h, 0, 0, (4, 8, 13, 14))
            if h == 1:
                swap_copy(gs[m].at[pl.ds(9 * own, 9)], outs[m], o_send.at[m], o_recv.at[m])

    @pl.when(z <= EARLY)
    def _():
        for i in range(MICROS):
            await_bytes(tin.at[i], act_recv.at[1, i])
        turned_s[...] = dot(tin[...].reshape(128, D), wt_jn[...]).reshape(MICROS, ROWS, D)
        join_partials()

    @pl.when(z == 0)
    def _():
        reduce_scatter((2,))

    def backward(i, _):
        @pl.when(deep)
        def _():
            for n, (lo, size) in enumerate(CHUNKS):
                await_bytes(cin.at[i, :, pl.ds(lo, size)], c_recv.at[i, n])
            e_s[rows(i), :] = cin[i]

        @pl.when(jnp.logical_not(deep))
        def _():
            @pl.when(z > EARLY)
            def _():
                await_bytes(tin.at[i], act_recv.at[1, i])
                turned_s[i] = dot(tin[i], wt_jn[...])

            for n, (lo, size) in enumerate(CHUNKS):
                await_bytes(cin.at[i, :, pl.ds(lo, size)], c_recv.at[i, n])
            e_s[rows(i), :] = (cin[i].astype(F32) + turned_s[i]).astype(BF)

        back_in = dot(e_s[rows(i), :], wt_dn[...])
        gp_s[rows(i), :] = (dg_s[i] * back_in).astype(BF)

        @pl.when(z > 0)
        def _():
            grad_normed = dot(gp_s[rows(i), :], wt_up[...]) * gain[0:1, :]
            inverse = inv_s[i][:, 0:1]
            normed = (u_s[i].astype(F32) - mean_s[i][:, 0:1]) * inverse
            first = jnp.mean(grad_normed, axis=-1, keepdims=True)
            second = jnp.mean(grad_normed * normed, axis=-1, keepdims=True)
            mixture = (grad_normed - first - normed * second) * inverse
            gout[i] = (e_s[rows(i), :].astype(F32) + mixture).astype(BF)

            @pl.when(deep)
            def _():
                remote(gout.at[i], tin.at[i], act_send.at[1, i], act_recv.at[1, i], mirror).start()
                for n, (lo, size) in enumerate(CHUNKS):
                    cols = pl.ds(lo, size)
                    cout[i, :, cols] = dot(gout[i], wt_jn[:, cols]).astype(BF)
                    remote(cout.at[i, :, cols], cin.at[i, :, cols], c_send.at[i, n], c_recv.at[i, n], z_down).start()

            @pl.when(jnp.logical_not(deep))
            def _():
                for n, (lo, size) in enumerate(CHUNKS):
                    cols = pl.ds(lo, size)
                    remote(gout.at[i, :, cols], cin.at[i, :, cols], c_send.at[i, n], c_recv.at[i, n], z_down).start()
        return 0

    lax.fori_loop(0, MICROS, backward, 0)

    at[...] = active_s[...].T
    partials(1, at, e_s, 288, True)
    lt[...] = scaled_s[...].T
    partials(0, lt, gp_s, 144, True)
    partials(1, at, e_s, 288, False)
    partials(0, lt, gp_s, 144, False)

    @pl.when(z > EARLY)
    def _():
        join_partials()

    @pl.when(z == 0)
    def _():
        reduce_scatter((1, 0))

    @pl.when(z > 0)
    def _():
        reduce_scatter((1, 0, 2))

    for m in (2, 1, 0):
        await_bytes(outs[m], o_recv.at[m])

    for m in range(3):
        swap_sent(ins[m], swap_send.at[m])
        swap_sent(outs[m], o_send.at[m])
        await_bytes(gs[m].at[pl.ds(0, 144)], x_send.at[m])
        await_bytes(gs[m].at[pl.ds(0, 135)], rs_send.at[m])
    swap_sent(st_gain, swap_send.at[3])

    for i in range(MICROS):
        for n, (lo, size) in enumerate(CHUNKS):
            piece = hout.at[i, :, pl.ds(lo, size)]

            @pl.when(gives_entry)
            def _():
                swap_sent(piece, io_send.at[0, i, n])

            @pl.when(gives_cot)
            def _():
                swap_sent(piece, io_send.at[1, i, n])

            @pl.when(z < 7)
            def _():
                await_bytes(piece, h_send.at[i, n])

            @pl.when(z > 0)
            def _():
                await_bytes(piece, c_send.at[i, n])

        @pl.when(jnp.logical_not(deep))
        def _():
            await_bytes(skout.at[i], act_send.at[0, i])

        @pl.when(deep)
        def _():
            await_bytes(gout.at[i], act_send.at[1, i])


def pick(steps, order, lat, table, out):
    row = rem(steps[pl.program_id(0)], 16)
    here = lax.broadcasted_iota(jnp.int32, (16, D), 0) == row
    moved = jnp.sum(jnp.where(here, table[...].astype(F32), 0.0), axis=0, keepdims=True)
    out[0] = (lat[0].astype(F32) + moved).astype(BF)


def widen(up, dn, jn, up_out, dn_out, jn_out):
    up_out[...] = up[...].astype(F32).reshape(up_out.shape)
    dn_out[...] = dn[...].astype(F32).reshape(dn_out.shape)
    jn_out[...] = jn[...].astype(F32).reshape(jn_out.shape)


def vm(*shape, dtype=BF):
    return pltpu.VMEM(shape, dtype)


def local(latents, time_table, timesteps, order, gains, w_up, w_down, w_join, cotangent):
    act = (MICROS, ROWS, D)
    tokens = MICROS * ROWS
    chunks = len(CHUNKS)
    dma = pltpu.SemaphoreType.DMA
    full = [vm(D, FFW), vm(FFW, D), vm(D, D)]
    scratch = (
        [vm(288, *u) for u in UNIT]
        + full
        + [vm(FFW, D), vm(D, FFW), vm(D, D)]
        + [vm(144, *u) for u in UNIT]
        + [vm(135, *u) for u in UNIT]
        + [vm(9, *u) for u in UNIT]
        + [vm(8, D, dtype=F32), vm(8, D, dtype=F32)]
        + [vm(*act) for _ in range(9)]
        + [
            vm(tokens, D), vm(tokens, FFW), vm(MICROS, ROWS, FFW, dtype=F32), vm(tokens, FFW), vm(tokens, D),
            vm(MICROS, ROWS, 128, dtype=F32), vm(MICROS, ROWS, 128, dtype=F32), vm(*act, dtype=F32),
            vm(tokens, D), vm(D, tokens), vm(FFW, tokens),
        ]
        + [
            dma((4,)), dma((4,)), dma((2, MICROS, chunks)), dma((3, 2, 16)), dma((3,)), dma((3,)), dma((3,)),
            dma((MICROS, chunks)), dma((MICROS, chunks)), dma((MICROS, chunks)), dma((MICROS, chunks)),
            dma((2, MICROS)), dma((2, MICROS)), dma((3,)), dma((3,)),
            dma((3, 2, 15)), dma((3,)), dma((3,)), dma((3,)),
        ]
    )
    spec = pl.BlockSpec(memory_space=pltpu.VMEM)
    micros, images, _ = latents.shape
    entry = pl.pallas_call(
        pick,
        grid_spec=pltpu.PrefetchScalarGridSpec(
            num_scalar_prefetch=2,
            grid=(micros,),
            in_specs=[
                pl.BlockSpec((1, images, D), lambda m, steps, order: (order[m], 0, 0)),
                pl.BlockSpec((16, D), lambda m, steps, order: (div(steps[m], 16), 0)),
            ],
            out_specs=pl.BlockSpec((1, images, D), lambda m, steps, order: (m, 0, 0)),
        ),
        out_shape=jax.ShapeDtypeStruct(latents.shape, BF),
        name="entries",
    )(timesteps, order, latents, time_table)
    sums = pl.pallas_call(
        kernel,
        out_shape=[jax.ShapeDtypeStruct((9,) + u, BF) for u in UNIT],
        in_specs=[spec] * 6,
        out_specs=[spec] * 3,
        scratch_shapes=scratch,
        compiler_params=pltpu.CompilerParams(
            collective_id=0, has_side_effects=True, vmem_limit_bytes=63 * 2**20
        ),
        name="blocks",
    )(w_up[0], w_down[0], w_join[0], gains, entry.reshape(act), cotangent.reshape(act))
    up, down, join = pl.pallas_call(
        widen,
        out_shape=[
            jax.ShapeDtypeStruct((36, 1, FFW), F32),
            jax.ShapeDtypeStruct((72, D), F32),
            jax.ShapeDtypeStruct((36, 1, D), F32),
        ],
        in_specs=[spec] * 3,
        out_specs=[spec] * 3,
        name="widen",
    )(*sums)
    return jnp.swapaxes(up, 0, 1), down[None], jnp.swapaxes(join, 0, 1)


def solution(mesh):
    in_specs = (
        P(None, "dp", None),
        P(),
        P(),
        P(),
        P("section", None),
        P("section", "dp", None),
        P("section", "dp", None),
        P("section", "dp", None),
        P(None, "dp", None),
    )
    out_specs = (P("section", "dp", None), P("section", "dp", None), P("section", "dp", None))
    return jax.shard_map(local, mesh=mesh, in_specs=in_specs, out_specs=out_specs, check_vma=False)
```

```python
import jax
import jax.numpy as jnp
from jax import lax
from jax.experimental import pallas as pl
from jax.experimental.pallas import tpu as pltpu
from jax.sharding import PartitionSpec as P

BF = jnp.bfloat16
F32 = jnp.float32
EPSILON = 1e-06
MESH = pl.DeviceIdType.MESH
D = 1152
FFW = 2304
ROWS = 32
GROUPS = 8
FEWER, MICROS = 3, 5
EARLY = 2
CHUNKS = ((0, 512), (512, 640))
PART = (((0, 5, 1), (5, 4, -1)), ((0, 4, -1), (4, 5, 1)), ((0, 4, 1), (4, 5, -1)))
UNIT = ((4, FFW), (8, D), (4, D))
GELU_C = 0.7978845608028654
GELU_A = 0.044715


def rem(a, b):
    return lax.rem(a, jnp.int32(b))


def div(a, b):
    return lax.div(a, jnp.int32(b))


def dot(a, b):
    return jnp.dot(a, b, preferred_element_type=F32)


def await_bytes(ref, sem):
    pltpu.make_async_copy(ref, ref, sem).wait()


def kernel(
    steps, order, up_in, dn_in, jn_in, gain_in, lat_in, time_in, cot_in,
    up_out, dn_out, jn_out,
    g_up, g_dn, g_jn, w_up, w_dn, w_jn, wt_up, wt_dn, wt_jn, rr_up, rr_dn, rr_jn,
    st_up, st_dn, st_jn, st_gain, gain, hin, skin, cin, tin, u_s, hout, skout, cout, gout,
    dg_s, mean_s, inv_s, turned_s, scaled_g, active_g, e_g, gp_g, left_g, right_g, scaled_t, active_t,
    time_sem, swap_sem, swap_send, io_send, ag_recv, ag_send, f_recv, f_send,
    h_recv, h_send, c_recv, c_send, act_recv, act_send, x_recv, x_send, rs_recv, rs_send, o_recv, o_send,
):
    q = lax.axis_index("dp")
    s = lax.axis_index("section")
    x, zl, y = div(q, 8), rem(div(q, 4), 2), rem(q, 4)
    zh, c = div(s, 2), rem(s, 2)
    z = 2 * zh + zl
    deep = z >= 4
    first, count = MICROS * (1 - c), FEWER + (MICROS - FEWER) * c
    first_there, count_there = MICROS * c, MICROS - (MICROS - FEWER) * c

    def device(xx, yy, zz, cc):
        return (xx * 8 + rem(zz, 2) * 4 + yy, div(zz, 2) * 2 + cc)

    partner = device(x, y, z, 1 - c)
    z_up = device(x, y, rem(z + 1, 8), c)
    z_down = device(x, y, rem(z + 7, 8), c)
    mirror = device(x, y, 7 - z, c)
    swap = device(x, y, 2 * zh + c, zl)
    stays = zl == c

    def along(axis, step):
        if axis == 0:
            return device(rem(x + 4 + step, 4), y, z, c)
        return device(x, rem(y + 4 + step, 4), z, c)

    other = device(x, y, 2 * zh + 1 - zl, 1 - c)

    def owner(h, d, i, j):
        back, side = 8 - d * i, 8 - d * j
        if h == 0:
            return rem(x + side, 4), rem(y + back, 4)
        return rem(x + back, 4), rem(y + side, 4)

    gs = (g_up, g_dn, g_jn)
    shared = (scaled_g, active_g, e_g, gp_g, left_g, right_g)
    rrs = (rr_up, rr_dn, rr_jn)
    outs = (up_out, dn_out, jn_out)

    def remote(src, dst, send, recv, dev):
        return pltpu.make_async_remote_copy(
            src_ref=src, dst_ref=dst, send_sem=send, recv_sem=recv, device_id=dev, device_id_type=MESH
        )

    def swap_copy(src, dst, send, recv):
        @pl.when(stays)
        def _():
            pltpu.make_async_copy(src, dst, recv).start()

        @pl.when(jnp.logical_not(stays))
        def _():
            remote(src, dst, send, recv, swap).start()

    def swap_sent(src, send):
        @pl.when(jnp.logical_not(stays))
        def _():
            await_bytes(src, send)

    ins = (st_up, st_dn, st_jn)
    st_up[...] = up_in[...].reshape((9,) + UNIT[0])
    st_dn[...] = dn_in[...].reshape((9,) + UNIT[1])
    st_jn[...] = jn_in[...].reshape((9,) + UNIT[2])
    st_gain[...] = jnp.broadcast_to(gain_in[...].astype(F32), (8, D))

    barrier = pltpu.get_barrier_semaphore()
    greet = [along(0, 1), along(0, -1), along(1, 1), along(1, -1), partner, z_up, z_down, mirror, other]
    for peer in greet:
        pl.semaphore_signal(barrier, inc=1, device_id=peer, device_id_type=MESH)
    pl.semaphore_wait(barrier, len(greet))

    for m in range(3):
        swap_copy(ins[m], gs[m].at[pl.ds(9 * q, 9)], swap_send.at[m], swap_sem.at[m])
    swap_copy(st_gain, gain, swap_send.at[3], swap_sem.at[3])
    gives_entry = (zh == 0) & (c == 0)
    gives_cot = (zh == 3) & (c == 1)

    def hand_in(src, dst, send, recv):
        for i in range(4):
            for n, (lo, size) in enumerate(CHUNKS):
                cols = pl.ds(lo, size)
                if i < FEWER:
                    swap_copy(src.at[i, :, cols], dst.at[i, :, cols], send.at[i, n], recv.at[i, n])
                    continue

                @pl.when(zl == 1)
                def _():
                    swap_copy(src.at[i, :, cols], dst.at[i, :, cols], send.at[i, n], recv.at[i, n])

                @pl.when(zl == 0)
                def _():
                    remote(
                        src.at[i, :, cols], dst.at[i - FEWER + 4, :, cols], send.at[i, n], recv.at[i - FEWER + 4, n],
                        device(x, y, 2 * zh + c, 1),
                    ).start()

    @pl.when(gives_entry)
    def _():
        table = rr_dn.at[pl.ds(0, time_in.shape[0])]
        pltpu.make_async_copy(time_in, table, time_sem).start()
        await_bytes(table, time_sem)
        row = lax.broadcasted_iota(jnp.int32, (8, D), 0)
        for m in range(2):
            block = rr_dn[div(steps[m], 8)].astype(F32)
            shift = jnp.sum(jnp.where(row == rem(steps[m], 8), block, 0.0), axis=0, keepdims=True)
            moved = lat_in[order[m]].astype(F32) + shift
            gout[2 * m:2 * m + 2] = moved.astype(BF).reshape(2, ROWS, D)
        hand_in(gout, hin, io_send.at[0], h_recv)

    @pl.when(gives_cot)
    def _():
        hand_in(cot_in, cin, io_send.at[1], c_recv)

    own = x * 8 + c * 4 + y

    def piece(m, h, i, j):
        off, cnt, d = PART[m][h]
        xx, yy = owner(h, d, i, j)
        return gs[m].at[pl.ds(9 * (xx * 8 + c * 4 + yy) + off, cnt)]

    def spread(m, ref, axis, step, recv):
        remote(ref, ref, ag_send.at[m], recv, along(axis, step)).start()

    def to_partner(m, ref):
        remote(ref, ref, f_send.at[m], f_recv.at[m], partner).start()

    def legs(weight):
        parts = [(weight, h) for h in range(2)]

        def first_axis(t, _):
            i = t + div(t, 2) * (5 - 2 * t)
            for m, h in parts:
                d = PART[m][h][2]
                f = 1 - h
                ref = piece(m, h, i, 0)

                @pl.when(i == 0)
                def _():
                    if h == 0:
                        await_bytes(gs[m].at[pl.ds(9 * own, 9)], swap_sem.at[m])
                    spread(m, ref, f, d, ag_recv.at[m, h, 1])
                    spread(m, ref, f, -d, ag_recv.at[m, h, 3])

                @pl.when(i > 0)
                def _():
                    await_bytes(ref, ag_recv.at[m, h, i])

                @pl.when(i == 1)
                def _():
                    spread(m, ref, f, d, ag_recv.at[m, h, 2])

                spread(m, ref, 1 - f, d, ag_recv.at[m, h, 4 + i])
                spread(m, ref, 1 - f, -d, ag_recv.at[m, h, 12 + i])
                to_partner(m, ref)
            return 0

        def second_axis(t, _):
            i = t + div(t, 2) * (5 - 2 * t)
            for m, h in parts:
                d = PART[m][h][2]
                ref = piece(m, h, i, 1)
                await_bytes(ref, ag_recv.at[m, h, 4 + i])
                spread(m, ref, h, d, ag_recv.at[m, h, 8 + i])
                to_partner(m, ref)
                ref = piece(m, h, i, 3)
                await_bytes(ref, ag_recv.at[m, h, 12 + i])
                to_partner(m, ref)
            return 0

        def last_hop(t, _):
            i = t + div(t, 2) * (5 - 2 * t)
            for m, h in parts:
                ref = piece(m, h, i, 2)
                await_bytes(ref, ag_recv.at[m, h, 8 + i])
                to_partner(m, ref)
            return 0

        return first_axis, second_axis, last_hop

    def conv(m):
        src, dst = gs[m], (w_up, w_dn, w_jn)[m]
        size = 4 * UNIT[m][0]

        def one(t, _):
            block = src[pl.ds(t * 4, 4)].reshape(size, UNIT[m][1])
            dst[pl.ds(pl.multiple_of(t * size, size), size), :] = block
            return 0

        lax.fori_loop(0, 72, one, 0, unroll=2)

    def gather(which):
        walks = [legs(m) for m in which]
        for leg in range(3):
            def all_of(t, _):
                for walk in walks:
                    walk[leg](t, 0)
                return 0

            lax.fori_loop(0, 4, all_of, 0)
        for m in which:
            await_bytes(gs[m].at[pl.ds(0, 144)], f_recv.at[m])
            conv(m)

    @pl.when(z <= 1)
    def _():
        gather((0, 1))

    @pl.when(z > 1)
    def _():
        gather((0, 1, 2))

    await_bytes(gain, swap_sem.at[3])

    def rows(i):
        return pl.ds(pl.multiple_of(i * ROWS, ROWS), ROWS)

    def transposes():
        def turn(src, dst, n):
            def one(i, _):
                block = pl.ds(pl.multiple_of(i * 128, 128), 128)
                dst[:, block] = src[block, :].T
                return 0

            lax.fori_loop(0, n, one, 0)

        turn(w_dn, wt_dn, 18)
        turn(w_up, wt_up, 9)
        turn(w_jn, wt_jn, 9)

    def show(kind, i):
        ref = shared[kind].at[rows(first + i)]
        remote(ref, ref, x_send.at[kind, first + i], x_recv.at[kind, first + i], partner).start()

    def seen(kind):
        def one(i, _):
            await_bytes(shared[kind].at[rows(first_there + i)], x_recv.at[kind, first_there + i])
            return 0

        lax.fori_loop(0, count_there, one, 0)

    def give_skip(i):
        skout[i] = dot(hout[i], w_jn[...]).astype(BF)
        remote(skout.at[i], skin.at[i], act_send.at[0, i], act_recv.at[0, i], mirror).start()

    def forward(i, _):
        mine = rows(first + i)
        for n, (lo, size) in enumerate(CHUNKS):
            await_bytes(hin.at[i, :, pl.ds(lo, size)], h_recv.at[i, n])

        @pl.when(deep)
        def _():
            joined = dot(hin[i], w_jn[...])
            await_bytes(skin.at[i], act_recv.at[0, i])
            u_s[i] = (joined + skin[i].astype(F32)).astype(BF)

        @pl.when(jnp.logical_not(deep))
        def _():
            u_s[i] = hin[i]

        values = u_s[i].astype(F32)
        middle = jnp.mean(values, axis=-1, keepdims=True)
        center = values - middle
        inverse = lax.rsqrt(jnp.mean(center * center, axis=-1, keepdims=True) + EPSILON)
        normed = center * inverse
        mean_s[i] = jnp.broadcast_to(middle, (ROWS, 128))
        inv_s[i] = jnp.broadcast_to(inverse, (ROWS, 128))
        scaled_g[mine, :] = (normed * gain[0:1, :]).astype(BF)
        pre = dot(scaled_g[mine, :], w_up[...])
        square = pre * pre
        bent = jnp.tanh(GELU_C * (pre + GELU_A * (square * pre)))
        grown = 0.5 * (1.0 + bent)
        active_g[mine, :] = (pre * grown).astype(BF)
        dg_s[i] = grown + 0.5 * pre * (1.0 - bent * bent) * (GELU_C * (1.0 + 3.0 * GELU_A * square))

        @pl.when(z < 7)
        def _():
            for n, (lo, size) in enumerate(CHUNKS):
                cols = pl.ds(lo, size)
                grown_by = dot(active_g[mine, :], w_dn[:, cols])
                hout[i, :, cols] = (u_s[i, :, cols].astype(F32) + grown_by).astype(BF)
                remote(hout.at[i, :, cols], hin.at[i, :, cols], h_send.at[i, n], h_recv.at[i, n], z_up).start()

        @pl.when(deep)
        def _():
            left_g[mine, :] = hin[i]

        @pl.when(jnp.logical_not(deep))
        def _():
            @pl.when(z > EARLY)
            def _():
                give_skip(i)

            left_g[mine, :] = hout[i]

        show(0, i)
        show(1, i)
        show(4, i)
        return 0

    for i in range(4):
        for n, (lo, size) in enumerate(CHUNKS):
            part = hout.at[i, :, pl.ds(lo, size)]
            for gives, kind in ((gives_entry, 0), (gives_cot, 1)):
                @pl.when(gives)
                def _():
                    if i < FEWER:
                        swap_sent(part, io_send.at[kind, i, n])
                        return

                    @pl.when(zl == 1)
                    def _():
                        swap_sent(part, io_send.at[kind, i, n])

                    @pl.when(zl == 0)
                    def _():
                        await_bytes(part, io_send.at[kind, i, n])

    @pl.when(deep)
    def _():
        transposes()

    lax.fori_loop(0, count, forward, 0)

    @pl.when(z <= 1)
    def _():
        gather((2,))

    @pl.when(z <= EARLY)
    def _():
        def one(i, _):
            give_skip(i)
            return 0

        lax.fori_loop(0, count, one, 0)

    @pl.when(jnp.logical_not(deep))
    def _():
        transposes()

    for m in range(3):
        await_bytes(gs[m].at[pl.ds(0, 135)], ag_send.at[m])
        await_bytes(gs[m].at[pl.ds(0, 144)], f_send.at[m])

    def partials(m, left, right, size):
        def one(j, _):
            t = 2 * j + c
            part = dot(left[pl.ds(pl.multiple_of(t * size, size), size), :], right[...])
            gs[m][pl.ds(36 * t, 36)] = part.reshape((36,) + UNIT[m]).astype(BF)
            return 0

        lax.fori_loop(0, 4, one, 0)

    def turn_activations():
        seen(0)
        seen(1)
        scaled_t[...] = scaled_g[...].T
        active_t[...] = active_g[...].T

    def join_partials():
        seen(4)
        seen(5)
        scaled_t[...] = left_g[...].T
        partials(2, scaled_t, right_g, 144)

    def piece_rows(m, h, i, j):
        off, cnt, d = PART[m][h]
        xx, yy = owner(h, d, i, j)
        return pl.ds(9 * (xx * 8 + c * 4 + yy) + off, cnt)

    def landing(m, h, n):
        cnt = PART[m][h][1]
        return pl.ds((0 if h == 0 else 15 * PART[m][0][1]) + n * cnt, cnt)

    def pass_on(m, h, mine, axis, step, n):
        remote(
            gs[m].at[mine], rrs[m].at[landing(m, h, n)], rs_send.at[m], rs_recv.at[m, h, n], along(axis, step)
        ).start()

    def launch(m):
        def one(i, _):
            for h in range(2):
                d = PART[m][h][2]
                pass_on(m, h, piece_rows(m, h, i, 2), h, -d, i)
                pass_on(m, h, piece_rows(m, h, i, 3), h, d, 4 + i)
            return 0

        lax.fori_loop(0, 4, one, 0)

    def collect(which):
        parts = [(m, h) for m in which for h in range(2)]

        def settle(m, h, i, j, slots):
            mine = piece_rows(m, h, i, j)
            total = gs[m][mine].astype(F32)
            for n in slots:
                spot = landing(m, h, n)
                await_bytes(rrs[m].at[spot], rs_recv.at[m, h, n])
                total = total + rrs[m][spot].astype(F32)
            gs[m][mine] = total.astype(BF)
            return mine

        def middle(i, _):
            for m, h in parts:
                pass_on(m, h, settle(m, h, i, 1, (i,)), h, -PART[m][h][2], 8 + i)
            return 0

        lax.fori_loop(0, 4, middle, 0)
        for m, h in parts:
            pass_on(m, h, settle(m, h, 2, 0, (6, 10)), 1 - h, -PART[m][h][2], 12)
        for m, h in parts:
            pass_on(m, h, settle(m, h, 3, 0, (7, 11)), 1 - h, PART[m][h][2], 14)
        for m, h in parts:
            pass_on(m, h, settle(m, h, 1, 0, (5, 9, 12)), 1 - h, -PART[m][h][2], 13)
        for m, h in parts:
            settle(m, h, 0, 0, (4, 8, 13, 14))
            if h == 1:
                swap_copy(gs[m].at[pl.ds(9 * own, 9)], outs[m], o_send.at[m], o_recv.at[m])

    @pl.when(z <= EARLY)
    def _():
        def one(i, _):
            await_bytes(tin.at[i], act_recv.at[1, i])
            right_g[rows(first + i), :] = tin[i]
            show(5, i)
            turned_s[i] = dot(tin[i], wt_jn[...])
            return 0

        lax.fori_loop(0, count, one, 0)
        join_partials()
        launch(2)
        turn_activations()

    @pl.when(z == 0)
    def _():
        collect((2,))

    def backward(i, _):
        mine = rows(first + i)

        @pl.when(deep)
        def _():
            for n, (lo, size) in enumerate(CHUNKS):
                await_bytes(cin.at[i, :, pl.ds(lo, size)], c_recv.at[i, n])
            e_g[mine, :] = cin[i]

        @pl.when(jnp.logical_not(deep))
        def _():
            @pl.when(z > EARLY)
            def _():
                await_bytes(tin.at[i], act_recv.at[1, i])
                right_g[mine, :] = tin[i]
                turned_s[i] = dot(tin[i], wt_jn[...])

            for n, (lo, size) in enumerate(CHUNKS):
                await_bytes(cin.at[i, :, pl.ds(lo, size)], c_recv.at[i, n])
            e_g[mine, :] = (cin[i].astype(F32) + turned_s[i]).astype(BF)

        back_in = dot(e_g[mine, :], wt_dn[...])
        gp_g[mine, :] = (dg_s[i] * back_in).astype(BF)

        @pl.when(z > 0)
        def _():
            grad_normed = dot(gp_g[mine, :], wt_up[...]) * gain[0:1, :]
            inverse = inv_s[i][:, 0:1]
            normed = (u_s[i].astype(F32) - mean_s[i][:, 0:1]) * inverse
            first = jnp.mean(grad_normed, axis=-1, keepdims=True)
            second = jnp.mean(grad_normed * normed, axis=-1, keepdims=True)
            mixture = (grad_normed - first - normed * second) * inverse
            gout[i] = (e_g[mine, :].astype(F32) + mixture).astype(BF)

            @pl.when(deep)
            def _():
                remote(gout.at[i], tin.at[i], act_send.at[1, i], act_recv.at[1, i], mirror).start()
                for n, (lo, size) in enumerate(CHUNKS):
                    cols = pl.ds(lo, size)
                    cout[i, :, cols] = dot(gout[i], wt_jn[:, cols]).astype(BF)
                    remote(cout.at[i, :, cols], cin.at[i, :, cols], c_send.at[i, n], c_recv.at[i, n], z_down).start()

            @pl.when(jnp.logical_not(deep))
            def _():
                for n, (lo, size) in enumerate(CHUNKS):
                    cols = pl.ds(lo, size)
                    remote(gout.at[i, :, cols], cin.at[i, :, cols], c_send.at[i, n], c_recv.at[i, n], z_down).start()

        show(2, i)
        show(3, i)

        @pl.when(deep)
        def _():
            right_g[mine, :] = gout[i]

        @pl.when(z > EARLY)
        def _():
            show(5, i)

        return 0

    lax.fori_loop(0, count, backward, 0)

    @pl.when(z > EARLY)
    def _():
        turn_activations()

    seen(2)
    partials(1, active_t, e_g, 288)
    launch(1)
    seen(3)
    partials(0, scaled_t, gp_g, 144)
    launch(0)

    @pl.when(z > EARLY)
    def _():
        join_partials()
        launch(2)

    @pl.when(z == 0)
    def _():
        collect((1, 0))

    @pl.when(z > 0)
    def _():
        collect((1, 0, 2))

    for m in (2, 1, 0):
        await_bytes(outs[m], o_recv.at[m])

    for m in range(3):
        swap_sent(ins[m], swap_send.at[m])
        swap_sent(outs[m], o_send.at[m])
        await_bytes(gs[m].at[pl.ds(0, 135)], rs_send.at[m])
    swap_sent(st_gain, swap_send.at[3])

    def all_sent(i, _):
        for n, (lo, size) in enumerate(CHUNKS):
            part = hout.at[i, :, pl.ds(lo, size)]

            @pl.when(z < 7)
            def _():
                await_bytes(part, h_send.at[i, n])

            @pl.when(z > 0)
            def _():
                await_bytes(part, c_send.at[i, n])

        @pl.when(jnp.logical_not(deep))
        def _():
            await_bytes(skout.at[i], act_send.at[0, i])

        @pl.when(deep)
        def _():
            await_bytes(gout.at[i], act_send.at[1, i])

        for kind in range(6):
            await_bytes(shared[kind].at[rows(first + i)], x_send.at[kind, first + i])
        return 0

    lax.fori_loop(0, count, all_sent, 0)


def widen(up, dn, jn, up_out, dn_out, jn_out):
    up_out[...] = up[...].astype(F32).reshape(up_out.shape)
    dn_out[...] = dn[...].astype(F32).reshape(dn_out.shape)
    jn_out[...] = jn[...].astype(F32).reshape(jn_out.shape)


def vm(*shape, dtype=BF):
    return pltpu.VMEM(shape, dtype)


def local(latents, time_table, timesteps, order, gains, w_up, w_down, w_join, cotangent):
    act = (MICROS, ROWS, D)
    tokens = GROUPS * ROWS
    chunks = len(CHUNKS)
    dma = pltpu.SemaphoreType.DMA
    full = [vm(D, FFW), vm(FFW, D), vm(D, D)]
    scratch = (
        [vm(288, *u) for u in UNIT]
        + full
        + [vm(FFW, D), vm(D, FFW), vm(D, D)]
        + [vm(135, *u) for u in UNIT]
        + [vm(9, *u) for u in UNIT]
        + [vm(8, D, dtype=F32), vm(8, D, dtype=F32)]
        + [vm(*act) for _ in range(9)]
        + [
            vm(MICROS, ROWS, FFW, dtype=F32), vm(MICROS, ROWS, 128, dtype=F32), vm(MICROS, ROWS, 128, dtype=F32),
            vm(*act, dtype=F32), vm(tokens, D), vm(tokens, FFW), vm(tokens, D), vm(tokens, FFW), vm(tokens, D),
            vm(tokens, D), vm(D, tokens), vm(FFW, tokens),
        ]
        + [
            dma, dma((4,)), dma((4,)), dma((2, 4, chunks)), dma((3, 2, 16)), dma((3,)), dma((3,)), dma((3,)),
            dma((MICROS, chunks)), dma((MICROS, chunks)), dma((MICROS, chunks)), dma((MICROS, chunks)),
            dma((2, MICROS)), dma((2, MICROS)), dma((6, GROUPS)), dma((6, GROUPS)),
            dma((3, 2, 15)), dma((3,)), dma((3,)), dma((3,)),
        ]
    )
    spec = pl.BlockSpec(memory_space=pltpu.VMEM)
    sums = pl.pallas_call(
        kernel,
        out_shape=[jax.ShapeDtypeStruct((9,) + u, BF) for u in UNIT],
        in_specs=[pl.BlockSpec(memory_space=pltpu.SMEM)] * 2 + [spec] * 5 + [pl.BlockSpec(memory_space=pl.ANY), spec],
        out_specs=[spec] * 3,
        scratch_shapes=scratch,
        compiler_params=pltpu.CompilerParams(
            collective_id=0, has_side_effects=True, vmem_limit_bytes=63 * 2**20
        ),
        name="blocks",
    )(timesteps, order, w_up[0], w_down[0], w_join[0], gains, latents, time_table.reshape(-1, 8, D), cotangent.reshape(4, ROWS, D))
    up, down, join = pl.pallas_call(
        widen,
        out_shape=[
            jax.ShapeDtypeStruct((36, 1, FFW), F32),
            jax.ShapeDtypeStruct((72, D), F32),
            jax.ShapeDtypeStruct((36, 1, D), F32),
        ],
        in_specs=[spec] * 3,
        out_specs=[spec] * 3,
        name="widen",
    )(*sums)
    return jnp.swapaxes(up, 0, 1), down[None], jnp.swapaxes(join, 0, 1)


def solution(mesh):
    in_specs = (
        P(None, "dp", None),
        P(),
        P(),
        P(),
        P("section", None),
        P("section", "dp", None),
        P("section", "dp", None),
        P("section", "dp", None),
        P(None, "dp", None),
    )
    out_specs = (P("section", "dp", None), P("section", "dp", None), P("section", "dp", None))
    return jax.shard_map(local, mesh=mesh, in_specs=in_specs, out_specs=out_specs, check_vma=False)
```

```python
import jax
import jax.numpy as jnp
from jax import lax
from jax.experimental import pallas as pl
from jax.experimental.pallas import tpu as pltpu
from jax.sharding import PartitionSpec as P

BF = jnp.bfloat16
F32 = jnp.float32
EPSILON = 1e-06
MESH = pl.DeviceIdType.MESH
D = 1152
FFW = 2304
ROWS = 32
GROUPS = 8
FEWER, MICROS = 3, 5
EARLY = 1
CHUNKS = ((0, 512), (512, 640))
PART = (((0, 5, 1), (5, 4, -1)), ((0, 4, -1), (4, 5, 1)), ((0, 4, 1), (4, 5, -1)))
UNIT = ((4, FFW), (8, D), (4, D))
GELU_C = 0.7978845608028654
GELU_A = 0.044715


def rem(a, b):
    return lax.rem(a, jnp.int32(b))


def div(a, b):
    return lax.div(a, jnp.int32(b))


def dot(a, b):
    return jnp.dot(a, b, preferred_element_type=F32)


def await_bytes(ref, sem):
    pltpu.make_async_copy(ref, ref, sem).wait()


def kernel(
    steps, order, up_in, dn_in, jn_in, gain_in, lat_in, time_in, cot_in,
    up_out, dn_out, jn_out,
    g_up, g_dn, g_jn, w_up, w_dn, w_jn, wt_up, wt_dn, wt_jn, rr_up, rr_dn, rr_jn,
    st_up, st_dn, st_jn, st_gain, gain, hin, skin, cin, tin, u_s, hout, skout, cout, gout,
    dg_s, mean_s, inv_s, turned_s, scaled_g, active_g, e_g, gp_g, left_g, right_g, scaled_t, active_t,
    time_sem, swap_sem, swap_send, io_send, ag_recv, ag_send, f_recv, f_send,
    h_recv, h_send, c_recv, c_send, act_recv, act_send, x_recv, x_send, rs_recv, rs_send, o_send,
):
    q = lax.axis_index("dp")
    s = lax.axis_index("section")
    x, zl, y = div(q, 8), rem(div(q, 4), 2), rem(q, 4)
    zh, c = div(s, 2), rem(s, 2)
    z = 2 * zh + zl
    deep = z >= 4
    first, count = MICROS * (1 - c), FEWER + (MICROS - FEWER) * c
    first_there, count_there = MICROS * c, MICROS - (MICROS - FEWER) * c

    def device(xx, yy, zz, cc):
        return (xx * 8 + rem(zz, 2) * 4 + yy, div(zz, 2) * 2 + cc)

    partner = device(x, y, z, 1 - c)
    z_up = device(x, y, rem(z + 1, 8), c)
    z_down = device(x, y, rem(z + 7, 8), c)
    mirror = device(x, y, 7 - z, c)
    swap = device(x, y, 2 * zh + c, zl)
    stays = zl == c

    def along(axis, step, plane=z, core=c):
        if axis == 0:
            return device(rem(x + 4 + step, 4), y, plane, core)
        return device(x, rem(y + 4 + step, 4), plane, core)

    def holder_along(axis, step):
        return along(axis, step, 2 * zh + c, zl)

    other = device(x, y, 2 * zh + 1 - zl, 1 - c)

    def owner(h, d, i, j):
        back, side = 8 - d * i, 8 - d * j
        if h == 0:
            return rem(x + side, 4), rem(y + back, 4)
        return rem(x + back, 4), rem(y + side, 4)

    gs = (g_up, g_dn, g_jn)
    shared = (scaled_g, active_g, e_g, gp_g, left_g, right_g)
    rrs = (rr_up, rr_dn, rr_jn)
    outs = (up_out, dn_out, jn_out)

    def remote(src, dst, send, recv, dev):
        return pltpu.make_async_remote_copy(
            src_ref=src, dst_ref=dst, send_sem=send, recv_sem=recv, device_id=dev, device_id_type=MESH
        )

    def swap_copy(src, dst, send, recv):
        @pl.when(stays)
        def _():
            pltpu.make_async_copy(src, dst, recv).start()

        @pl.when(jnp.logical_not(stays))
        def _():
            remote(src, dst, send, recv, swap).start()

    def swap_sent(src, send):
        @pl.when(jnp.logical_not(stays))
        def _():
            await_bytes(src, send)

    ins = (st_up, st_dn, st_jn)
    st_up[...] = up_in[...].reshape((9,) + UNIT[0])
    st_dn[...] = dn_in[...].reshape((9,) + UNIT[1])
    st_jn[...] = jn_in[...].reshape((9,) + UNIT[2])
    st_gain[...] = jnp.broadcast_to(gain_in[...].astype(F32), (8, D))

    barrier = pltpu.get_barrier_semaphore()
    greet = [along(0, 1), along(0, -1), along(1, 1), along(1, -1), partner, z_up, z_down, mirror, other]
    greet += [holder_along(0, 1), holder_along(0, -1), holder_along(1, 1), holder_along(1, -1)]
    for peer in greet:
        pl.semaphore_signal(barrier, inc=1, device_id=peer, device_id_type=MESH)
    pl.semaphore_wait(barrier, len(greet))

    for m in range(3):
        swap_copy(ins[m], gs[m].at[pl.ds(9 * q, 9)], swap_send.at[m], swap_sem.at[m])
    swap_copy(st_gain, gain, swap_send.at[3], swap_sem.at[3])
    gives_entry = (zh == 0) & (c == 0)
    gives_cot = (zh == 3) & (c == 1)

    def hand_in(src, dst, send, recv):
        for i in range(4):
            for n, (lo, size) in enumerate(CHUNKS):
                cols = pl.ds(lo, size)
                if i < FEWER:
                    swap_copy(src.at[i, :, cols], dst.at[i, :, cols], send.at[i, n], recv.at[i, n])
                    continue

                @pl.when(zl == 1)
                def _():
                    swap_copy(src.at[i, :, cols], dst.at[i, :, cols], send.at[i, n], recv.at[i, n])

                @pl.when(zl == 0)
                def _():
                    remote(
                        src.at[i, :, cols], dst.at[i - FEWER + 4, :, cols], send.at[i, n], recv.at[i - FEWER + 4, n],
                        device(x, y, 2 * zh + c, 1),
                    ).start()

    @pl.when(gives_entry)
    def _():
        table = rr_dn.at[pl.ds(0, time_in.shape[0])]
        pltpu.make_async_copy(time_in, table, time_sem).start()
        await_bytes(table, time_sem)
        row = lax.broadcasted_iota(jnp.int32, (8, D), 0)
        for m in range(2):
            block = rr_dn[div(steps[m], 8)].astype(F32)
            shift = jnp.sum(jnp.where(row == rem(steps[m], 8), block, 0.0), axis=0, keepdims=True)
            moved = lat_in[order[m]].astype(F32) + shift
            gout[2 * m:2 * m + 2] = moved.astype(BF).reshape(2, ROWS, D)
        hand_in(gout, hin, io_send.at[0], h_recv)

    @pl.when(gives_cot)
    def _():
        hand_in(cot_in, cin, io_send.at[1], c_recv)

    own = x * 8 + c * 4 + y

    def piece(m, h, i, j):
        off, cnt, d = PART[m][h]
        xx, yy = owner(h, d, i, j)
        return gs[m].at[pl.ds(9 * (xx * 8 + c * 4 + yy) + off, cnt)]

    def spread(m, ref, axis, step, recv):
        remote(ref, ref, ag_send.at[m], recv, along(axis, step)).start()

    def to_partner(m, ref):
        remote(ref, ref, f_send.at[m], f_recv.at[m], partner).start()

    def legs(weight):
        parts = [(weight, h) for h in range(2)]

        def first_axis(t, _):
            i = t + div(t, 2) * (5 - 2 * t)
            for m, h in parts:
                d = PART[m][h][2]
                f = 1 - h
                ref = piece(m, h, i, 0)

                @pl.when(i == 0)
                def _():
                    if h == 0:
                        await_bytes(gs[m].at[pl.ds(9 * own, 9)], swap_sem.at[m])
                    spread(m, ref, f, d, ag_recv.at[m, h, 1])
                    spread(m, ref, f, -d, ag_recv.at[m, h, 3])

                @pl.when(i > 0)
                def _():
                    await_bytes(ref, ag_recv.at[m, h, i])

                @pl.when(i == 1)
                def _():
                    spread(m, ref, f, d, ag_recv.at[m, h, 2])

                spread(m, ref, 1 - f, d, ag_recv.at[m, h, 4 + i])
                spread(m, ref, 1 - f, -d, ag_recv.at[m, h, 12 + i])
                to_partner(m, ref)
            return 0

        def second_axis(t, _):
            i = t + div(t, 2) * (5 - 2 * t)
            for m, h in parts:
                d = PART[m][h][2]
                ref = piece(m, h, i, 1)
                await_bytes(ref, ag_recv.at[m, h, 4 + i])
                spread(m, ref, h, d, ag_recv.at[m, h, 8 + i])
                to_partner(m, ref)
                ref = piece(m, h, i, 3)
                await_bytes(ref, ag_recv.at[m, h, 12 + i])
                to_partner(m, ref)
            return 0

        def last_hop(t, _):
            i = t + div(t, 2) * (5 - 2 * t)
            for m, h in parts:
                ref = piece(m, h, i, 2)
                await_bytes(ref, ag_recv.at[m, h, 8 + i])
                to_partner(m, ref)
            return 0

        return first_axis, second_axis, last_hop

    def conv(m):
        src, dst = gs[m], (w_up, w_dn, w_jn)[m]
        size = 4 * UNIT[m][0]

        def one(t, _):
            block = src[pl.ds(t * 4, 4)].reshape(size, UNIT[m][1])
            dst[pl.ds(pl.multiple_of(t * size, size), size), :] = block
            return 0

        lax.fori_loop(0, 72, one, 0, unroll=2)

    def gather(which):
        walks = [legs(m) for m in which]
        for leg in range(3):
            def all_of(t, _):
                for walk in walks:
                    walk[leg](t, 0)
                return 0

            lax.fori_loop(0, 4, all_of, 0)
        for m in which:
            await_bytes(gs[m].at[pl.ds(0, 144)], f_recv.at[m])
            conv(m)

    @pl.when(z <= 1)
    def _():
        gather((0, 1))

    @pl.when(z > 1)
    def _():
        gather((0, 1, 2))

    await_bytes(gain, swap_sem.at[3])

    def rows(i):
        return pl.ds(pl.multiple_of(i * ROWS, ROWS), ROWS)

    def transposes():
        def turn(src, dst, n):
            def one(i, _):
                block = pl.ds(pl.multiple_of(i * 128, 128), 128)
                dst[:, block] = src[block, :].T
                return 0

            lax.fori_loop(0, n, one, 0)

        turn(w_dn, wt_dn, 18)
        turn(w_up, wt_up, 9)
        turn(w_jn, wt_jn, 9)

    def show(kind, i):
        ref = shared[kind].at[rows(first + i)]
        remote(ref, ref, x_send.at[kind, first + i], x_recv.at[kind, first + i], partner).start()

    def seen(kind):
        def one(i, _):
            await_bytes(shared[kind].at[rows(first_there + i)], x_recv.at[kind, first_there + i])
            return 0

        lax.fori_loop(0, count_there, one, 0)

    def give_skip(i):
        skout[i] = dot(hout[i], w_jn[...]).astype(BF)
        remote(skout.at[i], skin.at[i], act_send.at[0, i], act_recv.at[0, i], mirror).start()

    def forward(i, _):
        mine = rows(first + i)
        for n, (lo, size) in enumerate(CHUNKS):
            await_bytes(hin.at[i, :, pl.ds(lo, size)], h_recv.at[i, n])

        @pl.when(deep)
        def _():
            joined = dot(hin[i], w_jn[...])
            await_bytes(skin.at[i], act_recv.at[0, i])
            u_s[i] = (joined + skin[i].astype(F32)).astype(BF)

        @pl.when(jnp.logical_not(deep))
        def _():
            u_s[i] = hin[i]

        values = u_s[i].astype(F32)
        middle = jnp.mean(values, axis=-1, keepdims=True)
        center = values - middle
        inverse = lax.rsqrt(jnp.mean(center * center, axis=-1, keepdims=True) + EPSILON)
        normed = center * inverse
        mean_s[i] = jnp.broadcast_to(middle, (ROWS, 128))
        inv_s[i] = jnp.broadcast_to(inverse, (ROWS, 128))
        scaled_g[mine, :] = (normed * gain[0:1, :]).astype(BF)
        pre = dot(scaled_g[mine, :], w_up[...])
        square = pre * pre
        bent = jnp.tanh(GELU_C * (pre + GELU_A * (square * pre)))
        grown = 0.5 * (1.0 + bent)
        active_g[mine, :] = (pre * grown).astype(BF)
        dg_s[i] = grown + 0.5 * pre * (1.0 - bent * bent) * (GELU_C * (1.0 + 3.0 * GELU_A * square))

        @pl.when(z < 7)
        def _():
            for n, (lo, size) in enumerate(CHUNKS):
                cols = pl.ds(lo, size)
                grown_by = dot(active_g[mine, :], w_dn[:, cols])
                hout[i, :, cols] = (u_s[i, :, cols].astype(F32) + grown_by).astype(BF)
                remote(hout.at[i, :, cols], hin.at[i, :, cols], h_send.at[i, n], h_recv.at[i, n], z_up).start()

        @pl.when(deep)
        def _():
            left_g[mine, :] = hin[i]

        @pl.when(jnp.logical_not(deep))
        def _():
            @pl.when(z > 2)
            def _():
                give_skip(i)

            left_g[mine, :] = hout[i]

        show(0, i)
        show(1, i)
        show(4, i)
        return 0

    def backward(i, _):
        mine = rows(first + i)

        @pl.when(deep)
        def _():
            for n, (lo, size) in enumerate(CHUNKS):
                await_bytes(cin.at[i, :, pl.ds(lo, size)], c_recv.at[i, n])
            e_g[mine, :] = cin[i]

        @pl.when(jnp.logical_not(deep))
        def _():
            @pl.when(z > EARLY)
            def _():
                await_bytes(tin.at[i], act_recv.at[1, i])
                right_g[mine, :] = tin[i]
                turned_s[i] = dot(tin[i], wt_jn[...])

            for n, (lo, size) in enumerate(CHUNKS):
                await_bytes(cin.at[i, :, pl.ds(lo, size)], c_recv.at[i, n])
            e_g[mine, :] = (cin[i].astype(F32) + turned_s[i]).astype(BF)

        back_in = dot(e_g[mine, :], wt_dn[...])
        gp_g[mine, :] = (dg_s[i] * back_in).astype(BF)

        @pl.when(z > 0)
        def _():
            grad_normed = dot(gp_g[mine, :], wt_up[...]) * gain[0:1, :]
            inverse = inv_s[i][:, 0:1]
            normed = (u_s[i].astype(F32) - mean_s[i][:, 0:1]) * inverse
            first = jnp.mean(grad_normed, axis=-1, keepdims=True)
            second = jnp.mean(grad_normed * normed, axis=-1, keepdims=True)
            mixture = (grad_normed - first - normed * second) * inverse
            gout[i] = (e_g[mine, :].astype(F32) + mixture).astype(BF)

            @pl.when(deep)
            def _():
                remote(gout.at[i], tin.at[i], act_send.at[1, i], act_recv.at[1, i], mirror).start()
                for n, (lo, size) in enumerate(CHUNKS):
                    cols = pl.ds(lo, size)
                    cout[i, :, cols] = dot(gout[i], wt_jn[:, cols]).astype(BF)
                    remote(cout.at[i, :, cols], cin.at[i, :, cols], c_send.at[i, n], c_recv.at[i, n], z_down).start()

            @pl.when(jnp.logical_not(deep))
            def _():
                for n, (lo, size) in enumerate(CHUNKS):
                    cols = pl.ds(lo, size)
                    remote(gout.at[i, :, cols], cin.at[i, :, cols], c_send.at[i, n], c_recv.at[i, n], z_down).start()

        show(2, i)
        show(3, i)

        @pl.when(deep)
        def _():
            right_g[mine, :] = gout[i]

        @pl.when(z > EARLY)
        def _():
            show(5, i)

        return 0

    for i in range(4):
        for n, (lo, size) in enumerate(CHUNKS):
            part = hout.at[i, :, pl.ds(lo, size)]
            for gives, kind in ((gives_entry, 0), (gives_cot, 1)):
                @pl.when(gives)
                def _():
                    if i < FEWER:
                        swap_sent(part, io_send.at[kind, i, n])
                        return

                    @pl.when(zl == 1)
                    def _():
                        swap_sent(part, io_send.at[kind, i, n])

                    @pl.when(zl == 0)
                    def _():
                        await_bytes(part, io_send.at[kind, i, n])

    @pl.when(deep)
    def _():
        transposes()

    @pl.when(z < 7)
    def _():
        lax.fori_loop(0, count, forward, 0)

    @pl.when(z == 7)
    def _():
        def both(i, _):
            forward(i, 0)
            return backward(i, 0)

        lax.fori_loop(0, count, both, 0)

    @pl.when(z <= 1)
    def _():
        gather((2,))

    @pl.when(z <= 2)
    def _():
        def one(i, _):
            give_skip(i)
            return 0

        lax.fori_loop(0, count, one, 0)

    @pl.when(jnp.logical_not(deep))
    def _():
        transposes()

    for m in range(3):
        await_bytes(gs[m].at[pl.ds(0, 135)], ag_send.at[m])
        await_bytes(gs[m].at[pl.ds(0, 144)], f_send.at[m])

    def partials(m, left, right, size):
        def one(j, _):
            t = 2 * j + c
            part = dot(left[pl.ds(pl.multiple_of(t * size, size), size), :], right[...])
            gs[m][pl.ds(36 * t, 36)] = part.reshape((36,) + UNIT[m]).astype(BF)
            return 0

        lax.fori_loop(0, 4, one, 0)

    def turn_activations():
        seen(0)
        seen(1)
        scaled_t[...] = scaled_g[...].T
        active_t[...] = active_g[...].T

    def join_partials():
        seen(4)
        seen(5)
        scaled_t[...] = left_g[...].T
        partials(2, scaled_t, right_g, 144)

    def piece_rows(m, h, i, j):
        off, cnt, d = PART[m][h]
        xx, yy = owner(h, d, i, j)
        return pl.ds(9 * (xx * 8 + c * 4 + yy) + off, cnt)

    def landing(m, h, n):
        cnt = PART[m][h][1]
        return pl.ds((0 if h == 0 else 16 * PART[m][0][1]) + n * cnt, cnt)

    def pass_on(m, h, mine, dev, n):
        remote(gs[m].at[mine], rrs[m].at[landing(m, h, n)], rs_send.at[m], rs_recv.at[m, h, n], dev).start()

    def launch(m):
        def one(t, _):
            i = rem(t + 2, 4)
            for h in range(2):
                d = PART[m][h][2]
                pass_on(m, h, piece_rows(m, h, i, 2), along(h, -d), i)
                pass_on(m, h, piece_rows(m, h, i, 3), along(h, d), 4 + i)
            return 0

        lax.fori_loop(0, 4, one, 0)

    def collect(which):
        parts = [(m, h) for m in which for h in range(2)]

        def settle(m, h, i, j, slots):
            mine = piece_rows(m, h, i, j)
            total = gs[m][mine].astype(F32)
            for n in slots:
                spot = landing(m, h, n)
                await_bytes(rrs[m].at[spot], rs_recv.at[m, h, n])
                total = total + rrs[m][spot].astype(F32)
            gs[m][mine] = total.astype(BF)
            return mine

        def middle(t, _):
            i = rem(t + 2, 4)
            for m, h in parts:
                pass_on(m, h, settle(m, h, i, 1, (i,)), along(h, -PART[m][h][2]), 8 + i)
            return 0

        lax.fori_loop(0, 4, middle, 0)
        for m, h in parts:
            pass_on(m, h, settle(m, h, 2, 0, (6, 10)), along(1 - h, -PART[m][h][2]), 12)
        for m, h in parts:
            pass_on(m, h, settle(m, h, 3, 0, (7, 11)), holder_along(1 - h, PART[m][h][2]), 14)
        for m, h in parts:
            mine = settle(m, h, 0, 0, (4, 8))
            swap_copy(gs[m].at[mine], rrs[m].at[landing(m, h, 15)], o_send.at[m, h], rs_recv.at[m, h, 15])
        for m, h in parts:
            pass_on(m, h, settle(m, h, 1, 0, (5, 9, 12)), holder_along(1 - h, -PART[m][h][2]), 13)

    @pl.when(z <= EARLY)
    def _():
        def one(i, _):
            await_bytes(tin.at[i], act_recv.at[1, i])
            right_g[rows(first + i), :] = tin[i]
            show(5, i)
            turned_s[i] = dot(tin[i], wt_jn[...])
            return 0

        lax.fori_loop(0, count, one, 0)
        join_partials()
        launch(2)
        turn_activations()

    @pl.when(z <= EARLY)
    def _():
        collect((2,))

    @pl.when(z < 7)
    def _():
        lax.fori_loop(0, count, backward, 0)

    @pl.when(z > EARLY)
    def _():
        turn_activations()

    seen(2)
    partials(1, active_t, e_g, 288)
    launch(1)
    seen(3)
    partials(0, scaled_t, gp_g, 144)
    launch(0)

    @pl.when(z > EARLY)
    def _():
        join_partials()
        launch(2)

    @pl.when(z <= EARLY)
    def _():
        collect((1, 0))

    @pl.when(z > EARLY)
    def _():
        collect((1, 0, 2))

    for m in (2, 1, 0):
        for h in range(2):
            off, cnt, _ = PART[m][h]
            total = 0.0
            for n in (14, 15, 13):
                spot = landing(m, h, n)
                await_bytes(rrs[m].at[spot], rs_recv.at[m, h, n])
                total = total + rrs[m][spot].astype(F32)
            outs[m][off:off + cnt] = total.astype(BF)

    for m in range(3):
        swap_sent(ins[m], swap_send.at[m])
        for h in range(2):
            swap_sent(rrs[m].at[landing(m, h, 15)], o_send.at[m, h])
        await_bytes(gs[m].at[pl.ds(0, 135)], rs_send.at[m])
    swap_sent(st_gain, swap_send.at[3])

    def all_sent(i, _):
        for n, (lo, size) in enumerate(CHUNKS):
            part = hout.at[i, :, pl.ds(lo, size)]

            @pl.when(z < 7)
            def _():
                await_bytes(part, h_send.at[i, n])

            @pl.when(z > 0)
            def _():
                await_bytes(part, c_send.at[i, n])

        @pl.when(jnp.logical_not(deep))
        def _():
            await_bytes(skout.at[i], act_send.at[0, i])

        @pl.when(deep)
        def _():
            await_bytes(gout.at[i], act_send.at[1, i])

        for kind in range(6):
            await_bytes(shared[kind].at[rows(first + i)], x_send.at[kind, first + i])
        return 0

    lax.fori_loop(0, count, all_sent, 0)


def widen(up, dn, jn, up_out, dn_out, jn_out):
    up_out[...] = up[...].astype(F32).reshape(up_out.shape)
    dn_out[...] = dn[...].astype(F32).reshape(dn_out.shape)
    jn_out[...] = jn[...].astype(F32).reshape(jn_out.shape)


def vm(*shape, dtype=BF):
    return pltpu.VMEM(shape, dtype)


def local(latents, time_table, timesteps, order, gains, w_up, w_down, w_join, cotangent):
    act = (MICROS, ROWS, D)
    tokens = GROUPS * ROWS
    chunks = len(CHUNKS)
    dma = pltpu.SemaphoreType.DMA
    full = [vm(D, FFW), vm(FFW, D), vm(D, D)]
    scratch = (
        [vm(288, *u) for u in UNIT]
        + full
        + [vm(FFW, D), vm(D, FFW), vm(D, D)]
        + [vm(144, *u) for u in UNIT]
        + [vm(9, *u) for u in UNIT]
        + [vm(8, D, dtype=F32), vm(8, D, dtype=F32)]
        + [vm(*act) for _ in range(9)]
        + [
            vm(MICROS, ROWS, FFW, dtype=F32), vm(MICROS, ROWS, 128, dtype=F32), vm(MICROS, ROWS, 128, dtype=F32),
            vm(*act, dtype=F32), vm(tokens, D), vm(tokens, FFW), vm(tokens, D), vm(tokens, FFW), vm(tokens, D),
            vm(tokens, D), vm(D, tokens), vm(FFW, tokens),
        ]
        + [
            dma, dma((4,)), dma((4,)), dma((2, 4, chunks)), dma((3, 2, 16)), dma((3,)), dma((3,)), dma((3,)),
            dma((MICROS, chunks)), dma((MICROS, chunks)), dma((MICROS, chunks)), dma((MICROS, chunks)),
            dma((2, MICROS)), dma((2, MICROS)), dma((6, GROUPS)), dma((6, GROUPS)),
            dma((3, 2, 16)), dma((3,)), dma((3, 2)),
        ]
    )
    spec = pl.BlockSpec(memory_space=pltpu.VMEM)
    sums = pl.pallas_call(
        kernel,
        out_shape=[jax.ShapeDtypeStruct((9,) + u, BF) for u in UNIT],
        in_specs=[pl.BlockSpec(memory_space=pltpu.SMEM)] * 2 + [spec] * 5 + [pl.BlockSpec(memory_space=pl.ANY), spec],
        out_specs=[spec] * 3,
        scratch_shapes=scratch,
        compiler_params=pltpu.CompilerParams(
            collective_id=0, has_side_effects=True, vmem_limit_bytes=63 * 2**20
        ),
        name="blocks",
    )(timesteps, order, w_up[0], w_down[0], w_join[0], gains, latents, time_table.reshape(-1, 8, D), cotangent.reshape(4, ROWS, D))
    up, down, join = pl.pallas_call(
        widen,
        out_shape=[
            jax.ShapeDtypeStruct((36, 1, FFW), F32),
            jax.ShapeDtypeStruct((72, D), F32),
            jax.ShapeDtypeStruct((36, 1, D), F32),
        ],
        in_specs=[spec] * 3,
        out_specs=[spec] * 3,
        name="widen",
    )(*sums)
    return jnp.swapaxes(up, 0, 1), down[None], jnp.swapaxes(join, 0, 1)


def solution(mesh):
    in_specs = (
        P(None, "dp", None),
        P(),
        P(),
        P(),
        P("section", None),
        P("section", "dp", None),
        P("section", "dp", None),
        P("section", "dp", None),
        P(None, "dp", None),
    )
    out_specs = (P("section", "dp", None), P("section", "dp", None), P("section", "dp", None))
    return jax.shard_map(local, mesh=mesh, in_specs=in_specs, out_specs=out_specs, check_vma=False)
```

```python
import jax
import jax.numpy as jnp
from jax import lax
from jax.experimental import pallas as pl
from jax.experimental.pallas import tpu as pltpu
from jax.sharding import PartitionSpec as P

BF = jnp.bfloat16
F32 = jnp.float32
EPSILON = 1e-06
MESH = pl.DeviceIdType.MESH
D = 1152
FFW = 2304
ROWS = 32
GROUPS = 8
FEWER, MICROS = 3, 5
EARLY = 1
CHUNKS = ((0, 512), (512, 640))
PART = (((0, 5, 1), (5, 4, -1)), ((0, 4, -1), (4, 5, 1)), ((0, 4, 1), (4, 5, -1)))
UNIT = ((4, FFW), (8, D), (4, D))
GELU_C = 0.7978845608028654
GELU_A = 0.044715


def rem(a, b):
    return lax.rem(a, jnp.int32(b))


def div(a, b):
    return lax.div(a, jnp.int32(b))


def dot(a, b):
    return jnp.dot(a, b, preferred_element_type=F32)


def await_bytes(ref, sem):
    pltpu.make_async_copy(ref, ref, sem).wait()


def kernel(
    steps, order, up_in, dn_in, jn_in, gain_in, lat_in, time_in, cot_in,
    up_out, dn_out, jn_out,
    g_up, g_dn, g_jn, w_up, w_dn, w_jn, wt_up, wt_dn, wt_jn, rr_up, rr_dn, rr_jn,
    st_up, st_dn, st_jn, st_gain, gain, hin, skin, cin, tin, u_s, hout, skout, cout, gout,
    dg_s, mean_s, inv_s, turned_s, scaled_g, active_g, e_g, gp_g, left_g, right_g, scaled_t, active_t,
    time_sem, swap_sem, swap_send, io_send, ag_recv, ag_send, f_recv, f_send,
    h_recv, h_send, c_recv, c_send, act_recv, act_send, x_recv, x_send, rs_recv, rs_send, o_send,
):
    q = lax.axis_index("dp")
    s = lax.axis_index("section")
    x, zl, y = div(q, 8), rem(div(q, 4), 2), rem(q, 4)
    zh, c = div(s, 2), rem(s, 2)
    z = 2 * zh + zl
    deep = z >= 4
    first, count = MICROS * (1 - c), FEWER + (MICROS - FEWER) * c
    first_there, count_there = MICROS * c, MICROS - (MICROS - FEWER) * c

    def device(xx, yy, zz, cc):
        return (xx * 8 + rem(zz, 2) * 4 + yy, div(zz, 2) * 2 + cc)

    partner = device(x, y, z, 1 - c)
    z_up = device(x, y, rem(z + 1, 8), c)
    z_down = device(x, y, rem(z + 7, 8), c)
    mirror = device(x, y, 7 - z, c)
    swap = device(x, y, 2 * zh + c, zl)
    stays = zl == c

    def along(axis, step, plane=z, core=c):
        if axis == 0:
            return device(rem(x + 4 + step, 4), y, plane, core)
        return device(x, rem(y + 4 + step, 4), plane, core)

    def holder_along(axis, step):
        return along(axis, step, 2 * zh + c, zl)

    other = device(x, y, 2 * zh + 1 - zl, 1 - c)

    def owner(h, d, i, j):
        back, side = 8 - d * i, 8 - d * j
        if h == 0:
            return rem(x + side, 4), rem(y + back, 4)
        return rem(x + back, 4), rem(y + side, 4)

    gs = (g_up, g_dn, g_jn)
    shared = (scaled_g, active_g, e_g, gp_g, left_g, right_g)
    rrs = (rr_up, rr_dn, rr_jn)
    outs = (up_out, dn_out, jn_out)

    def remote(src, dst, send, recv, dev):
        return pltpu.make_async_remote_copy(
            src_ref=src, dst_ref=dst, send_sem=send, recv_sem=recv, device_id=dev, device_id_type=MESH
        )

    def swap_copy(src, dst, send, recv):
        @pl.when(stays)
        def _():
            pltpu.make_async_copy(src, dst, recv).start()

        @pl.when(jnp.logical_not(stays))
        def _():
            remote(src, dst, send, recv, swap).start()

    def swap_sent(src, send):
        @pl.when(jnp.logical_not(stays))
        def _():
            await_bytes(src, send)

    barrier = pltpu.get_barrier_semaphore()
    greet = [along(0, 1), along(0, -1), along(1, 1), along(1, -1), partner, z_up, z_down, mirror, other]
    greet += [holder_along(0, 1), holder_along(0, -1), holder_along(1, 1), holder_along(1, -1)]
    for peer in greet:
        pl.semaphore_signal(barrier, inc=1, device_id=peer, device_id_type=MESH)

    ins = (st_up, st_dn, st_jn)
    st_up[...] = up_in[...].reshape((9,) + UNIT[0])
    st_dn[...] = dn_in[...].reshape((9,) + UNIT[1])
    st_jn[...] = jn_in[...].reshape((9,) + UNIT[2])
    st_gain[...] = jnp.broadcast_to(gain_in[...].astype(F32), (8, D))

    pl.semaphore_wait(barrier, len(greet))

    for m in range(3):
        swap_copy(ins[m], gs[m].at[pl.ds(9 * q, 9)], swap_send.at[m], swap_sem.at[m])
    swap_copy(st_gain, gain, swap_send.at[3], swap_sem.at[3])
    gives_entry = (zh == 0) & (c == 0)
    gives_cot = (zh == 3) & (c == 1)

    def hand_in(src, dst, send, recv):
        for i in range(4):
            for n, (lo, size) in enumerate(CHUNKS):
                cols = pl.ds(lo, size)
                if i < FEWER:
                    swap_copy(src.at[i, :, cols], dst.at[i, :, cols], send.at[i, n], recv.at[i, n])
                    continue

                @pl.when(zl == 1)
                def _():
                    swap_copy(src.at[i, :, cols], dst.at[i, :, cols], send.at[i, n], recv.at[i, n])

                @pl.when(zl == 0)
                def _():
                    remote(
                        src.at[i, :, cols], dst.at[i - FEWER + 4, :, cols], send.at[i, n], recv.at[i - FEWER + 4, n],
                        device(x, y, 2 * zh + c, 1),
                    ).start()

    @pl.when(gives_entry)
    def _():
        table = rr_dn.at[pl.ds(0, time_in.shape[0])]
        pltpu.make_async_copy(time_in, table, time_sem).start()
        await_bytes(table, time_sem)
        row = lax.broadcasted_iota(jnp.int32, (8, D), 0)
        for m in range(2):
            block = rr_dn[div(steps[m], 8)].astype(F32)
            shift = jnp.sum(jnp.where(row == rem(steps[m], 8), block, 0.0), axis=0, keepdims=True)
            moved = lat_in[order[m]].astype(F32) + shift
            gout[2 * m:2 * m + 2] = moved.astype(BF).reshape(2, ROWS, D)
        hand_in(gout, hin, io_send.at[0], h_recv)

    @pl.when(gives_cot)
    def _():
        hand_in(cot_in, cin, io_send.at[1], c_recv)

    own = x * 8 + c * 4 + y

    def piece(m, h, i, j):
        off, cnt, d = PART[m][h]
        xx, yy = owner(h, d, i, j)
        return gs[m].at[pl.ds(9 * (xx * 8 + c * 4 + yy) + off, cnt)]

    def spread(m, ref, axis, step, recv):
        remote(ref, ref, ag_send.at[m], recv, along(axis, step)).start()

    def to_partner(m, ref):
        remote(ref, ref, f_send.at[m], f_recv.at[m], partner).start()

    def legs(weight):
        parts = [(weight, h) for h in range(2)]

        def first_axis(t, _):
            i = t + div(t, 2) * (5 - 2 * t)
            for m, h in parts:
                d = PART[m][h][2]
                f = 1 - h
                ref = piece(m, h, i, 0)

                @pl.when(i == 0)
                def _():
                    if h == 0:
                        await_bytes(gs[m].at[pl.ds(9 * own, 9)], swap_sem.at[m])
                    spread(m, ref, f, d, ag_recv.at[m, h, 1])
                    spread(m, ref, f, -d, ag_recv.at[m, h, 3])

                @pl.when(i > 0)
                def _():
                    await_bytes(ref, ag_recv.at[m, h, i])

                @pl.when(i == 1)
                def _():
                    spread(m, ref, f, d, ag_recv.at[m, h, 2])

                spread(m, ref, 1 - f, d, ag_recv.at[m, h, 4 + i])
                spread(m, ref, 1 - f, -d, ag_recv.at[m, h, 12 + i])
                to_partner(m, ref)
            return 0

        def second_axis(t, _):
            i = t + div(t, 2) * (5 - 2 * t)
            for m, h in parts:
                d = PART[m][h][2]
                ref = piece(m, h, i, 1)
                await_bytes(ref, ag_recv.at[m, h, 4 + i])
                spread(m, ref, h, d, ag_recv.at[m, h, 8 + i])
                to_partner(m, ref)
                ref = piece(m, h, i, 3)
                await_bytes(ref, ag_recv.at[m, h, 12 + i])
                to_partner(m, ref)
            return 0

        def last_hop(t, _):
            i = t + div(t, 2) * (5 - 2 * t)
            for m, h in parts:
                ref = piece(m, h, i, 2)
                await_bytes(ref, ag_recv.at[m, h, 8 + i])
                to_partner(m, ref)
            return 0

        return first_axis, second_axis, last_hop

    def conv(m):
        src, dst = gs[m], (w_up, w_dn, w_jn)[m]
        size = 4 * UNIT[m][0]

        def one(t, _):
            block = src[pl.ds(t * 4, 4)].reshape(size, UNIT[m][1])
            dst[pl.ds(pl.multiple_of(t * size, size), size), :] = block
            return 0

        lax.fori_loop(0, 72, one, 0, unroll=2)

    def gather(which):
        walks = [legs(m) for m in which]
        for leg in range(3):
            def all_of(t, _):
                for walk in walks:
                    walk[leg](t, 0)
                return 0

            lax.fori_loop(0, 4, all_of, 0)
        for m in which:
            await_bytes(gs[m].at[pl.ds(0, 144)], f_recv.at[m])
            conv(m)

    @pl.when(z <= 1)
    def _():
        gather((0, 1))

    @pl.when(z > 1)
    def _():
        gather((0, 1, 2))

    await_bytes(gain, swap_sem.at[3])

    def rows(i):
        return pl.ds(pl.multiple_of(i * ROWS, ROWS), ROWS)

    def transposes():
        def turn(src, dst, n):
            def one(i, _):
                block = pl.ds(pl.multiple_of(i * 128, 128), 128)
                dst[:, block] = src[block, :].T
                return 0

            lax.fori_loop(0, n, one, 0)

        turn(w_dn, wt_dn, 18)
        turn(w_up, wt_up, 9)
        turn(w_jn, wt_jn, 9)

    def show(kind, i):
        ref = shared[kind].at[rows(first + i)]
        remote(ref, ref, x_send.at[kind, first + i], x_recv.at[kind, first + i], partner).start()

    def seen(kind):
        def one(i, _):
            await_bytes(shared[kind].at[rows(first_there + i)], x_recv.at[kind, first_there + i])
            return 0

        lax.fori_loop(0, count_there, one, 0)

    def give_skip(i):
        skout[i] = dot(hout[i], w_jn[...]).astype(BF)
        remote(skout.at[i], skin.at[i], act_send.at[0, i], act_recv.at[0, i], mirror).start()

    def forward(i, _):
        mine = rows(first + i)
        for n, (lo, size) in enumerate(CHUNKS):
            await_bytes(hin.at[i, :, pl.ds(lo, size)], h_recv.at[i, n])

        @pl.when(deep)
        def _():
            joined = dot(hin[i], w_jn[...])
            await_bytes(skin.at[i], act_recv.at[0, i])
            u_s[i] = (joined + skin[i].astype(F32)).astype(BF)

        @pl.when(jnp.logical_not(deep))
        def _():
            u_s[i] = hin[i]

        values = u_s[i].astype(F32)
        middle = jnp.mean(values, axis=-1, keepdims=True)
        center = values - middle
        inverse = lax.rsqrt(jnp.mean(center * center, axis=-1, keepdims=True) + EPSILON)
        normed = center * inverse
        mean_s[i] = jnp.broadcast_to(middle, (ROWS, 128))
        inv_s[i] = jnp.broadcast_to(inverse, (ROWS, 128))
        scaled_g[mine, :] = (normed * gain[0:1, :]).astype(BF)
        pre = dot(scaled_g[mine, :], w_up[...])
        square = pre * pre
        bent = jnp.tanh(GELU_C * (pre + GELU_A * (square * pre)))
        grown = 0.5 * (1.0 + bent)
        active_g[mine, :] = (pre * grown).astype(BF)
        dg_s[i] = grown + 0.5 * pre * (1.0 - bent * bent) * (GELU_C * (1.0 + 3.0 * GELU_A * square))

        @pl.when(z < 7)
        def _():
            for n, (lo, size) in enumerate(CHUNKS):
                cols = pl.ds(lo, size)
                grown_by = dot(active_g[mine, :], w_dn[:, cols])
                hout[i, :, cols] = (u_s[i, :, cols].astype(F32) + grown_by).astype(BF)
                remote(hout.at[i, :, cols], hin.at[i, :, cols], h_send.at[i, n], h_recv.at[i, n], z_up).start()

        @pl.when(deep)
        def _():
            left_g[mine, :] = hin[i]

        @pl.when(jnp.logical_not(deep))
        def _():
            @pl.when(z > 2)
            def _():
                give_skip(i)

            left_g[mine, :] = hout[i]

        show(0, i)
        show(1, i)
        show(4, i)
        return 0

    def backward(i, _):
        mine = rows(first + i)

        @pl.when(deep)
        def _():
            for n, (lo, size) in enumerate(CHUNKS):
                await_bytes(cin.at[i, :, pl.ds(lo, size)], c_recv.at[i, n])
            e_g[mine, :] = cin[i]

        @pl.when(jnp.logical_not(deep))
        def _():
            @pl.when(z > EARLY)
            def _():
                await_bytes(tin.at[i], act_recv.at[1, i])
                right_g[mine, :] = tin[i]
                turned_s[i] = dot(tin[i], wt_jn[...])

            for n, (lo, size) in enumerate(CHUNKS):
                await_bytes(cin.at[i, :, pl.ds(lo, size)], c_recv.at[i, n])
            e_g[mine, :] = (cin[i].astype(F32) + turned_s[i]).astype(BF)

        back_in = dot(e_g[mine, :], wt_dn[...])
        gp_g[mine, :] = (dg_s[i] * back_in).astype(BF)

        @pl.when(z > 0)
        def _():
            grad_normed = dot(gp_g[mine, :], wt_up[...]) * gain[0:1, :]
            inverse = inv_s[i][:, 0:1]
            normed = (u_s[i].astype(F32) - mean_s[i][:, 0:1]) * inverse
            first = jnp.mean(grad_normed, axis=-1, keepdims=True)
            second = jnp.mean(grad_normed * normed, axis=-1, keepdims=True)
            mixture = (grad_normed - first - normed * second) * inverse
            gout[i] = (e_g[mine, :].astype(F32) + mixture).astype(BF)

            @pl.when(deep)
            def _():
                remote(gout.at[i], tin.at[i], act_send.at[1, i], act_recv.at[1, i], mirror).start()
                for n, (lo, size) in enumerate(CHUNKS):
                    cols = pl.ds(lo, size)
                    cout[i, :, cols] = dot(gout[i], wt_jn[:, cols]).astype(BF)
                    remote(cout.at[i, :, cols], cin.at[i, :, cols], c_send.at[i, n], c_recv.at[i, n], z_down).start()

            @pl.when(jnp.logical_not(deep))
            def _():
                for n, (lo, size) in enumerate(CHUNKS):
                    cols = pl.ds(lo, size)
                    remote(gout.at[i, :, cols], cin.at[i, :, cols], c_send.at[i, n], c_recv.at[i, n], z_down).start()

        show(2, i)
        show(3, i)

        @pl.when(deep)
        def _():
            right_g[mine, :] = gout[i]

        @pl.when(z > EARLY)
        def _():
            show(5, i)

        return 0

    for i in range(4):
        for n, (lo, size) in enumerate(CHUNKS):
            part = hout.at[i, :, pl.ds(lo, size)]
            for gives, kind in ((gives_entry, 0), (gives_cot, 1)):
                @pl.when(gives)
                def _():
                    if i < FEWER:
                        swap_sent(part, io_send.at[kind, i, n])
                        return

                    @pl.when(zl == 1)
                    def _():
                        swap_sent(part, io_send.at[kind, i, n])

                    @pl.when(zl == 0)
                    def _():
                        await_bytes(part, io_send.at[kind, i, n])

    @pl.when(deep)
    def _():
        transposes()

    @pl.when(z < 7)
    def _():
        lax.fori_loop(0, count, forward, 0)

    @pl.when(z == 7)
    def _():
        def both(i, _):
            forward(i, 0)
            return backward(i, 0)

        lax.fori_loop(0, count, both, 0)

    @pl.when(z <= 1)
    def _():
        gather((2,))

    @pl.when(z <= 2)
    def _():
        def one(i, _):
            give_skip(i)
            return 0

        lax.fori_loop(0, count, one, 0)

    @pl.when(jnp.logical_not(deep))
    def _():
        transposes()

    for m in range(3):
        await_bytes(gs[m].at[pl.ds(0, 135)], ag_send.at[m])
        await_bytes(gs[m].at[pl.ds(0, 144)], f_send.at[m])

    def turn_activations():
        seen(0)
        seen(1)
        scaled_t[...] = scaled_g[...].T
        active_t[...] = active_g[...].T

    def join_partials():
        seen(4)
        seen(5)
        scaled_t[...] = left_g[...].T
        partials(2, scaled_t, right_g, 144)

    def piece_rows(m, h, i, j):
        off, cnt, d = PART[m][h]
        xx, yy = owner(h, d, i, j)
        return pl.ds(9 * (xx * 8 + c * 4 + yy) + off, cnt)

    def landing(m, h, n):
        cnt = PART[m][h][1]
        return pl.ds((0 if h == 0 else 16 * PART[m][0][1]) + n * cnt, cnt)

    def pass_on(m, h, mine, dev, n):
        remote(gs[m].at[mine], rrs[m].at[landing(m, h, n)], rs_send.at[m], rs_recv.at[m, h, n], dev).start()

    def partials(m, left, right, size):
        def far(h, i):
            pass_on(m, h, piece_rows(m, h, i, 2), along(h, -PART[m][h][2]), i)

        def near(h, i):
            pass_on(m, h, piece_rows(m, h, i, 3), along(h, PART[m][h][2]), 4 + i)

        def one(step, _):
            t = 2 * rem(x + 2 + step, 4) + c
            part = dot(left[pl.ds(pl.multiple_of(t * size, size), size), :], right[...])
            gs[m][pl.ds(36 * t, 36)] = part.reshape((36,) + UNIT[m]).astype(BF)
            i = rem(16 - PART[m][1][2] * (step + 2), 4)
            far(1, i)
            near(1, i)

            @pl.when(step == 0)
            def _():
                for i in (2, 3, 0, 1):
                    far(0, i)

            @pl.when(step == 2 + PART[m][0][2])
            def _():
                for i in (2, 3, 0, 1):
                    near(0, i)

            return 0

        lax.fori_loop(0, 4, one, 0)

    def collect(which):
        parts = [(m, h) for m in which for h in range(2)]

        def settle(m, h, i, j, slots):
            mine = piece_rows(m, h, i, j)
            total = gs[m][mine].astype(F32)
            for n in slots:
                spot = landing(m, h, n)
                await_bytes(rrs[m].at[spot], rs_recv.at[m, h, n])
                total = total + rrs[m][spot].astype(F32)
            gs[m][mine] = total.astype(BF)
            return mine

        def middle(t, _):
            i = rem(t + 2, 4)
            for m, h in parts:
                pass_on(m, h, settle(m, h, i, 1, (i,)), along(h, -PART[m][h][2]), 8 + i)
            return 0

        lax.fori_loop(0, 4, middle, 0)
        for m, h in parts:
            pass_on(m, h, settle(m, h, 2, 0, (6, 10)), along(1 - h, -PART[m][h][2]), 12)
        for m, h in parts:
            pass_on(m, h, settle(m, h, 3, 0, (7, 11)), holder_along(1 - h, PART[m][h][2]), 14)
        for m, h in parts:
            mine = settle(m, h, 0, 0, (4, 8))
            swap_copy(gs[m].at[mine], rrs[m].at[landing(m, h, 15)], o_send.at[m, h], rs_recv.at[m, h, 15])
        for m, h in parts:
            pass_on(m, h, settle(m, h, 1, 0, (5, 9, 12)), holder_along(1 - h, -PART[m][h][2]), 13)

    @pl.when(z <= EARLY)
    def _():
        def one(i, _):
            await_bytes(tin.at[i], act_recv.at[1, i])
            right_g[rows(first + i), :] = tin[i]
            show(5, i)
            turned_s[i] = dot(tin[i], wt_jn[...])
            return 0

        lax.fori_loop(0, count, one, 0)
        join_partials()
        turn_activations()

    @pl.when(z <= EARLY)
    def _():
        collect((2,))

    @pl.when(z < 7)
    def _():
        lax.fori_loop(0, count, backward, 0)

    @pl.when(z > EARLY)
    def _():
        turn_activations()

    seen(2)
    partials(1, active_t, e_g, 288)
    seen(3)
    partials(0, scaled_t, gp_g, 144)

    @pl.when(z > EARLY)
    def _():
        join_partials()

    @pl.when(z <= EARLY)
    def _():
        collect((1, 0))

    @pl.when(z > EARLY)
    def _():
        collect((1, 0, 2))

    for m in (2, 1, 0):
        for h in range(2):
            off, cnt, _ = PART[m][h]
            total = 0.0
            for n in (14, 15, 13):
                spot = landing(m, h, n)
                await_bytes(rrs[m].at[spot], rs_recv.at[m, h, n])
                total = total + rrs[m][spot].astype(F32)
            outs[m][off:off + cnt] = total.astype(BF)

    for m in range(3):
        swap_sent(ins[m], swap_send.at[m])
        for h in range(2):
            swap_sent(rrs[m].at[landing(m, h, 15)], o_send.at[m, h])
        await_bytes(gs[m].at[pl.ds(0, 135)], rs_send.at[m])
    swap_sent(st_gain, swap_send.at[3])

    def all_sent(i, _):
        for n, (lo, size) in enumerate(CHUNKS):
            part = hout.at[i, :, pl.ds(lo, size)]

            @pl.when(z < 7)
            def _():
                await_bytes(part, h_send.at[i, n])

            @pl.when(z > 0)
            def _():
                await_bytes(part, c_send.at[i, n])

        @pl.when(jnp.logical_not(deep))
        def _():
            await_bytes(skout.at[i], act_send.at[0, i])

        @pl.when(deep)
        def _():
            await_bytes(gout.at[i], act_send.at[1, i])

        for kind in range(6):
            await_bytes(shared[kind].at[rows(first + i)], x_send.at[kind, first + i])
        return 0

    lax.fori_loop(0, count, all_sent, 0)


def widen(up, dn, jn, up_out, dn_out, jn_out):
    up_out[...] = up[...].astype(F32).reshape(up_out.shape)
    dn_out[...] = dn[...].astype(F32).reshape(dn_out.shape)
    jn_out[...] = jn[...].astype(F32).reshape(jn_out.shape)


def vm(*shape, dtype=BF):
    return pltpu.VMEM(shape, dtype)


def local(latents, time_table, timesteps, order, gains, w_up, w_down, w_join, cotangent):
    act = (MICROS, ROWS, D)
    tokens = GROUPS * ROWS
    chunks = len(CHUNKS)
    dma = pltpu.SemaphoreType.DMA
    full = [vm(D, FFW), vm(FFW, D), vm(D, D)]
    scratch = (
        [vm(288, *u) for u in UNIT]
        + full
        + [vm(FFW, D), vm(D, FFW), vm(D, D)]
        + [vm(144, *u) for u in UNIT]
        + [vm(9, *u) for u in UNIT]
        + [vm(8, D, dtype=F32), vm(8, D, dtype=F32)]
        + [vm(*act) for _ in range(9)]
        + [
            vm(MICROS, ROWS, FFW, dtype=F32), vm(MICROS, ROWS, 128, dtype=F32), vm(MICROS, ROWS, 128, dtype=F32),
            vm(*act, dtype=F32), vm(tokens, D), vm(tokens, FFW), vm(tokens, D), vm(tokens, FFW), vm(tokens, D),
            vm(tokens, D), vm(D, tokens), vm(FFW, tokens),
        ]
        + [
            dma, dma((4,)), dma((4,)), dma((2, 4, chunks)), dma((3, 2, 16)), dma((3,)), dma((3,)), dma((3,)),
            dma((MICROS, chunks)), dma((MICROS, chunks)), dma((MICROS, chunks)), dma((MICROS, chunks)),
            dma((2, MICROS)), dma((2, MICROS)), dma((6, GROUPS)), dma((6, GROUPS)),
            dma((3, 2, 16)), dma((3,)), dma((3, 2)),
        ]
    )
    spec = pl.BlockSpec(memory_space=pltpu.VMEM)
    sums = pl.pallas_call(
        kernel,
        out_shape=[jax.ShapeDtypeStruct((9,) + u, BF) for u in UNIT],
        in_specs=[pl.BlockSpec(memory_space=pltpu.SMEM)] * 2 + [spec] * 5 + [pl.BlockSpec(memory_space=pl.ANY), spec],
        out_specs=[spec] * 3,
        scratch_shapes=scratch,
        compiler_params=pltpu.CompilerParams(
            collective_id=0, has_side_effects=True, vmem_limit_bytes=63 * 2**20
        ),
        name="blocks",
    )(timesteps, order, w_up[0], w_down[0], w_join[0], gains, latents, time_table.reshape(-1, 8, D), cotangent.reshape(4, ROWS, D))
    up, down, join = pl.pallas_call(
        widen,
        out_shape=[
            jax.ShapeDtypeStruct((36, 1, FFW), F32),
            jax.ShapeDtypeStruct((72, D), F32),
            jax.ShapeDtypeStruct((36, 1, D), F32),
        ],
        in_specs=[spec] * 3,
        out_specs=[spec] * 3,
        name="widen",
    )(*sums)
    return jnp.swapaxes(up, 0, 1), down[None], jnp.swapaxes(join, 0, 1)


def solution(mesh):
    in_specs = (
        P(None, "dp", None),
        P(),
        P(),
        P(),
        P("section", None),
        P("section", "dp", None),
        P("section", "dp", None),
        P("section", "dp", None),
        P(None, "dp", None),
    )
    out_specs = (P("section", "dp", None), P("section", "dp", None), P("section", "dp", None))
    return jax.shard_map(local, mesh=mesh, in_specs=in_specs, out_specs=out_specs, check_vma=False)
```
